256 devices in a mesh: ex: 4 (over y), par: 64 (over z, x, core).
Axes of the slice: x: 4, y: 4, z: 8, core: 2. Of those that a mesh axis runs over, the one named last changes fastest.
Arguments:
- train_grads: bfloat16 [128, 524288], P('ex', 'par'), may hold values from -17 to 17
- val_grads: bfloat16 [32, 524288], P('ex', 'par'), may hold values from -17 to 17
- first_moment: float32 [524288], P('par'), may hold values from -0.6 to 0.6
- second_moment: float32 [524288], P('par'), may hold values from 0.01 to 1
- row_codes: int32 [524288], P('par'), may hold values from 1 to 1864135
- col_codes: int32 [8192], replicated, may hold values from 1 to 1073741823
- mix_offset: int32 [1], replicated, may hold values from 0 to 999999
Outputs:
- train_features: float32 [128, 8192], P('ex', 'par')
- scores: float32 [128, 32], P('ex')
The draws below stay inside these ranges and needn't reach their ends.
All inputs are finite; a program needn't handle non-finite values.
Results may differ from the reference program's by a relative error of at most 0.0029.
Values may be sent and summed in bfloat16 or wider, within the bound.
A program may use at most 64 MiB of HBM per device.

```python
import math
import jax
import jax.numpy as jnp
from jax import lax

K = 8192
P_SIZE = 524288
TRAIN = 128
VALS = 32


def shared_direction(key):
    return jnp.clip(jax.random.normal(jax.random.fold_in(key, 99), (P_SIZE,), jnp.float32), -4.0, 4.0)


def combine_rows(key, own, common, weight_common, weight_own, lowest):
    rows = own.shape[0]
    scales = jnp.exp(jax.random.uniform(jax.random.fold_in(key, 7), (rows, 1), jnp.float32, math.log(lowest), math.log(3.0)))
    return (scales * (weight_common * common[None, :] + weight_own * own)).astype(jnp.bfloat16)


def draw_train_grads(key, part):
    common = shared_direction(key)
    key = jax.random.fold_in(key, 1)
    own = jnp.clip(jax.random.normal(key, (TRAIN, P_SIZE), jnp.float32), -4.0, 4.0)
    return combine_rows(key, own, common, 0.7, 0.71, 0.3)


def draw_val_grads(key, part):
    common = shared_direction(key)
    key = jax.random.fold_in(key, 2)
    own = jnp.clip(jax.random.normal(key, (VALS, P_SIZE), jnp.float32), -4.0, 4.0)
    return combine_rows(key, own, common, 0.7, 0.71, 0.3)


def touch_ends(array, stream_key, smallest, largest):
    longest = array.shape.index(max(array.shape))
    spots = []
    for shift in (0, 1):
        where = [jax.random.randint(jax.random.fold_in(stream_key, axis), (), 0, length) for axis, length in enumerate(array.shape)]
        where[longest] = (where[longest] + shift) % array.shape[longest]
        spots.append(tuple(where))
    return array.at[spots[0]].set(smallest).at[spots[1]].set(largest)


def block_levels(key, shape, cuts, low, high):
    def one(dim, blocks):
        heights = jax.random.uniform(jax.random.fold_in(jax.random.fold_in(key, 6), dim), (blocks,), jnp.float32, low / len(cuts), high / len(cuts))
        return jnp.repeat(jnp.exp(heights), shape[dim] // blocks).reshape((-1,) + (1,) * (len(shape) - dim - 1))

    factor_of = one(*cuts[0])
    for cut in cuts[1:]:
        factor_of = factor_of * one(*cut)
    return factor_of


def scatter_about(rng, shape, width, bound, cuts=(), held_as=jnp.bfloat16):
    factor_of = block_levels(rng, shape, cuts, -0.22, 0.18) if cuts else 1.0
    result = jax.random.normal(rng, shape, jnp.float32) * width * factor_of
    return jnp.minimum(jnp.maximum(result, -bound), bound).astype(held_as)


def setup_inputs(seed: int = 0) -> dict:
    splits = jax.random.split(jax.random.key(seed), 8)
    train_grads = draw_train_grads(jax.random.fold_in(splits[7], 71), 0)
    val_grads = draw_val_grads(jax.random.fold_in(splits[7], 71), 0)
    first_moment = scatter_about(splits[2], (P_SIZE,), 0.1, 0.6, ((0, 64),), jnp.float32)
    second_moment = jnp.clip(jnp.exp(math.log(1.0) - 4.6051702 * jax.random.uniform(splits[3], (P_SIZE,), jnp.float32) ** block_levels(splits[3], (P_SIZE,), ((0, 64),), -0.2, 0.2)), 0.01, 1.0)
    row_codes = touch_ends(jax.random.randint(splits[4], (P_SIZE,), 1, 1864136), jax.random.fold_in(splits[4], 1), 1, 1864135).astype(jnp.int32)
    col_codes = touch_ends(jax.random.randint(splits[5], (K,), 1, 2 ** 30), jax.random.fold_in(splits[5], 1), 1, (2 ** 30) - 1).astype(jnp.int32)
    mix_offset = jax.random.randint(splits[6], (1,), 0, 1000000).astype(jnp.int32)
    return dict(train_grads=train_grads, val_grads=val_grads, first_moment=first_moment, second_moment=second_moment, row_codes=row_codes, col_codes=col_codes, mix_offset=mix_offset)


def make_tile(row_part, col_part, offset_code):
    mixed = row_part[:, None] * col_part[None, :] + offset_code
    mixed = mixed ^ mixed >> 15
    mixed = mixed * 739982445
    bits = mixed >> 16 & 1
    return (2 * bits - 1).astype(jnp.bfloat16)

def normalize(values):
    inverse = lax.rsqrt(lax.optimization_barrier(jnp.mean(values * values, axis=1)) + 1e-06)
    return values * inverse[:, None]

def reference(train_grads, val_grads, first_moment, second_moment, row_codes, col_codes, mix_offset):
    grads = train_grads.astype(jnp.float32)
    moment_one = 0.9 * first_moment[None, :] + 0.1 * grads
    moment_two = 0.999 * second_moment[None, :] + 0.001 * grads * grads
    adam_dir = (moment_one / (jnp.sqrt(moment_two) + 1e-08)).astype(jnp.bfloat16)
    stacked = jnp.concatenate([adam_dir, val_grads], axis=0)
    block_rows = math.gcd(P_SIZE, 4096)
    offset_code = mix_offset[0]

    def add_block(total, index):
        first = index * block_rows
        row_part = lax.dynamic_slice_in_dim(row_codes, first, block_rows)
        grad_part = lax.dynamic_slice_in_dim(stacked, first, block_rows, 1)
        tile = make_tile(row_part, col_codes, offset_code)
        return (total + jnp.dot(grad_part, tile, preferred_element_type=jnp.float32), None)
    start_total = jnp.zeros((TRAIN + VALS, K), jnp.float32)
    total, unused = lax.scan(add_block, start_total, jnp.arange(P_SIZE // block_rows, dtype=jnp.int32))
    features = total * (1.0 / math.sqrt(P_SIZE))
    train_features = normalize(features[:TRAIN])
    val_norm = normalize(features[TRAIN:])
    scores = jnp.dot(train_features, val_norm.T, precision=lax.Precision.HIGHEST) / K
    return (train_features, scores)
```

```python
import functools
import math

import jax
import jax.numpy as jnp
from jax import lax
from jax.experimental import pallas as pl
from jax.experimental.pallas import tpu as pltpu
from jax.sharding import PartitionSpec as P

K = 8192
P_SIZE = 524288
MESH = pl.DeviceIdType.MESH
LANES = 128
NX = 4
NC = 2
TRAIN_ROWS = 32
VAL_ROWS = 8
SIGN_FACTOR = ((739982445 << 15) + 2**31) % 2**32 - 2**31
X_LAG = 2
Y_LAG = 3


def make_entries(row_b, cols, offset, dest, depth):
    step = 128
    for first in range(0, depth, step):
        rows = row_b[first : first + step, :]
        for half, col in enumerate(cols):
            mixed = rows * col + offset
            mixed = mixed ^ (mixed >> 15)
            mixed = mixed * SIGN_FACTOR
            dest[first : first + step, half * LANES : (half + 1) * LANES] = jnp.where(
                mixed < 0, jnp.bfloat16(1), jnp.bfloat16(-1)
            )


def kernel(
    ny, nz, gen_first,
    train_ref, val_ref, m1_ref, m2_ref, rows_ref, cols_ref, off_ref,
    feat_ref, scores_ref,
    row_b, train_in, val_out, val_in, g_ref, tiles,
    core_out, core_in, own, x_out, x_in, x_sum, y_out, y_in, y_own, z_out, z_in,
    g1_out, g1_in, g2_out, g2_in,
    in_send, in_recv, in_local, core_send, core_recv, x_send, x_recv, y_send, y_recv, z_send, z_recv,
    g1_send, g1_recv, g2_send, g2_recv,
):
    y0 = lax.axis_index("ex")
    q0 = lax.axis_index("par")
    c0 = lax.rem(q0, NC)
    x0 = lax.rem(q0 // NC, NX)
    z0 = q0 // (NC * NX)
    depth = row_b.shape[0]
    all_train = ny * TRAIN_ROWS
    all_val = ny * VAL_ROWS
    all_rows = all_train + all_val
    piece = TRAIN_ROWS + all_val

    def par_of(z, x, c):
        return (z * NX + x) * NC + c

    peers = [(y0, par_of(z0, x0, 1 - c0))]
    peers += [(y0, par_of(z0, lax.rem(x0 + d, NX), c)) for d in range(1, NX) for c in (c0, 1 - c0)]
    peers += [(lax.rem(y0 + d, ny), q0) for d in range(1, ny)]
    peers += [(y0, par_of(lax.rem(z0 + d, nz), x0, c0)) for d in range(1, nz)]
    barrier = pltpu.get_barrier_semaphore()
    for peer in peers:
        pl.semaphore_signal(barrier, inc=1, device_id=peer, device_id_type=MESH)

    half = depth // 2
    for d in range(ny):
        e = lax.rem(y0 + d, ny)
        upper = val_ref[:, pl.ds(pl.multiple_of(e * depth, LANES), half)].astype(jnp.float32)
        lower = val_ref[:, pl.ds(pl.multiple_of(e * depth + half, LANES), half)].astype(jnp.float32)
        stacked = jnp.concatenate([upper, lower], axis=0).astype(jnp.bfloat16)
        if d == 0:
            val_in[y0] = stacked
        else:
            val_out[d - 1] = stacked

    def remote(src, dst, send, recv, peer):
        return pltpu.make_async_remote_copy(
            src_ref=src, dst_ref=dst, send_sem=send, recv_sem=recv, device_id=peer, device_id_type=MESH
        )

    def train_copy(d, slot):
        e = lax.rem(y0 + d, ny)
        return remote(
            train_ref.at[:, pl.ds(pl.multiple_of(e * depth, LANES), depth)],
            train_in.at[slot], in_send.at[0, d - 1], in_recv.at[0, d - 1], (e, q0),
        )

    def val_copy(d, slot):
        e = lax.rem(y0 + d, ny)
        return remote(val_out.at[d - 1], val_in.at[slot], in_send.at[1, d - 1], in_recv.at[1, d - 1], (e, q0))

    pl.semaphore_wait(barrier, len(peers))
    for d in range(1, ny):
        train_copy(d, y0).start()
        val_copy(d, y0).start()
    local_copy = pltpu.make_async_copy(
        train_ref.at[:, pl.ds(pl.multiple_of(y0 * depth, LANES), depth)], train_in.at[y0], in_local
    )
    local_copy.start()

    groups = depth // LANES
    codes = rows_ref[pl.ds(pl.multiple_of(y0 * groups, groups), groups), :].T
    for j in range(groups):
        row_b[j * LANES : (j + 1) * LANES, :] = jnp.broadcast_to(codes[:, j : j + 1], (LANES, LANES))
    offset = off_ref[0]

    order = (2, 1, 3, 0)

    def tile_features(t, step_in_chunk):
        z = lax.rem(z0 + 1 + t, nz)
        x = lax.rem(x0 + step_in_chunk, NX)
        base = par_of(z, x, 0) * LANES
        mine = cols_ref[:, pl.ds(pl.multiple_of(base + c0 * LANES, LANES), LANES)]
        other = cols_ref[:, pl.ds(pl.multiple_of(base + (1 - c0) * LANES, LANES), LANES)]
        return mine, other

    def distance(k):
        return jnp.where(k == 0, 2, jnp.where(k == 1, 1, jnp.where(k == 2, 3, 0)))

    def generate(t):
        cols = tile_features(t // NX, distance(lax.rem(t, NX)))
        make_entries(row_b, cols, offset, tiles.at[t], depth)

    lax.fori_loop(0, gen_first, lambda t, c: (generate(t), c)[1], 0)

    local_copy.wait()
    for d in range(1, ny):
        source = lax.rem(y0 + ny - d, ny)
        train_copy(d, source).wait_recv()
        val_copy(d, source).wait_recv()

    def fill(j, carry):
        vals = [[], []]
        at = pl.ds(pl.multiple_of(j * LANES, LANES), LANES)
        for e in range(ny):
            both = val_in[e, :, at].astype(jnp.float32)
            vals[0].append(both[:VAL_ROWS])
            vals[1].append(both[VAL_ROWS:])
        for h in range(2):
            block = j + h * (groups // 2)
            here = pl.ds(pl.multiple_of(block * LANES, LANES), LANES)
            there = pl.ds(pl.multiple_of(y0 * depth + block * LANES, LANES), LANES)
            m1 = 0.9 * m1_ref[:, there]
            m2 = 0.999 * m2_ref[:, there]
            for e in range(ny):
                g = train_in[e, :, here].astype(jnp.float32)
                direction = (m1 + 0.1 * g) / (jnp.sqrt(m2 + 0.001 * g * g) + 1e-08)
                g_ref[block, e * TRAIN_ROWS : (e + 1) * TRAIN_ROWS, :] = direction.astype(jnp.bfloat16)
            g_ref[block, all_train:all_rows, :] = jnp.concatenate(vals[h], axis=0).astype(jnp.bfloat16)
        return carry

    lax.fori_loop(0, groups // 2, fill, 0)

    sibling = (y0, par_of(z0, x0, 1 - c0))

    def core_copy(pair):
        return remote(core_out.at[pair], core_in.at[pair], core_send.at[pair], core_recv.at[pair], sibling)

    def x_copy(i, d):
        peer = (y0, par_of(z0, lax.rem(x0 + d, NX), c0))
        return remote(x_out.at[i, d - 1], x_in.at[i, d - 1], x_send.at[i, d - 1], x_recv.at[i, d - 1], peer)

    def y_copy(i, d):
        peer = (lax.rem(y0 + d, ny), q0)
        return remote(y_out.at[i, d - 1], y_in.at[i, d - 1], y_send.at[i, d - 1], y_recv.at[i, d - 1], peer)

    def z_copy(i):
        peer = (y0, par_of(lax.rem(z0 + 1 + i, nz), x0, c0))
        return remote(z_out.at[i], z_in.at[i], z_send.at[i], z_recv.at[i], peer)

    def multiply(pair):
        lhs = jnp.concatenate([g_ref[b] for b in range(groups)], axis=1)
        for k in range(2):
            part = jnp.dot(lhs, tiles[pair * 2 + k], preferred_element_type=jnp.float32)
            own[pair, k] = part[:, :LANES]
            core_out[pair, k] = part[:, LANES:]
        core_copy(pair).start()

    def after_core(i, second):
        pair = i * 2 + second
        core_copy(pair).wait_recv()
        for k in range(2):
            d = order[second * 2 + k]
            total = own[pair, k] + core_in[pair, k]
            if d == 0:
                own[pair, k] = total
            else:
                x_out[i, d - 1] = total.astype(jnp.bfloat16)
                x_copy(i, d).start()

    def after_x(i):
        for d in range(1, NX):
            x_copy(i, d).wait_recv()
        total = own[i * 2 + 1, 1]
        for d in range(1, NX):
            total = total + x_in[i, d - 1].astype(jnp.float32)
        x_sum[...] = total
        vals = total[all_train:]
        for d in range(1, ny):
            e = lax.rem(y0 + d, ny)
            trains = x_sum[pl.ds(pl.multiple_of(e * TRAIN_ROWS, TRAIN_ROWS), TRAIN_ROWS), :]
            y_out[i, d - 1] = jnp.concatenate([trains, vals], axis=0).astype(jnp.bfloat16)
            y_copy(i, d).start()
        trains = x_sum[pl.ds(pl.multiple_of(y0 * TRAIN_ROWS, TRAIN_ROWS), TRAIN_ROWS), :]
        y_own[i] = jnp.concatenate([trains, vals], axis=0)

    def y_total(i):
        for d in range(1, ny):
            y_copy(i, d).wait_recv()
        total = y_own[i]
        for d in range(1, ny):
            total = total + y_in[i, d - 1].astype(jnp.float32)
        return total

    def after_y(i):
        z_out[i] = y_total(i)
        z_copy(i).start()

    def chunk(i, gen):
        for second in range(2):
            if gen:
                generate(gen_first + i * 2 + second)
            multiply(i * 2 + second)
            if second == 0:
                @pl.when(i >= 1)
                def _():
                    after_core(i - 1, 1)

                @pl.when(i >= X_LAG)
                def _():
                    after_x(i - X_LAG)
            else:
                after_core(i, 0)

                @pl.when(i >= Y_LAG)
                def _():
                    after_y(i - Y_LAG)

    with_gen = (nz * NX - gen_first) // 2
    lax.fori_loop(0, with_gen, lambda i, c: (chunk(i, True), c)[1], 0)
    lax.fori_loop(with_gen, nz, lambda i, c: (chunk(i, False), c)[1], 0)
    after_core(nz - 1, 1)
    for i in range(nz - X_LAG, nz):
        after_x(i)
    for i in range(nz - Y_LAG, nz - 1):
        after_y(i)
    total = y_total(nz - 1)
    for i in range(nz - 1):
        z_copy(i).wait_recv()
        total = total + z_in[i]

    total = total * (1.0 / math.sqrt(P_SIZE))
    trains, vals = total[:TRAIN_ROWS], total[TRAIN_ROWS:]
    fold = LANES // all_val
    wide = jnp.concatenate([vals] * fold, axis=0)
    dims = (((1,), (1,)), ((), ()))
    inner = lax.dot_general(trains, wide, dims, precision=lax.Precision.HIGHEST, preferred_element_type=jnp.float32)
    val_sq = lax.dot_general(
        jnp.ones((8, LANES), jnp.float32), wide * wide, dims,
        precision=lax.Precision.HIGHEST, preferred_element_type=jnp.float32,
    )
    train_sq = jnp.broadcast_to(jnp.sum(trains * trains, axis=1, keepdims=True), (TRAIN_ROWS, LANES))
    block = lax.broadcasted_iota(jnp.int32, (8, LANES), 1) // all_val

    def packed(a):
        out = a[:8]
        for b in range(1, TRAIN_ROWS // 8):
            out = jnp.where(block == b, a[b * 8 : (b + 1) * 8], out)
        return out

    def share(message, out_ref, in_ref, send, recv, targets):
        out_ref[...] = message
        copies = [
            remote(out_ref, in_ref.at[n], send.at[n], recv.at[n], target) for n, target in enumerate(targets)
        ]
        for copy in copies:
            copy.start()
        for n, copy in enumerate(copies):
            copy.wait_recv()
            message = message + in_ref[n]
        return message, copies

    message = jnp.concatenate([packed(inner), packed(train_sq), val_sq], axis=0)
    near = [(y0, par_of(z0, lax.rem(x0 + d, NX), c)) for d in range(NX) for c in (c0, 1 - c0)][1:]
    message, copies1 = share(message, g1_out, g1_in, g1_send, g1_recv, near)
    far = [(y0, par_of(lax.rem(z0 + d, nz), x0, c0)) for d in range(1, nz)]
    message, copies2 = share(message, g2_out, g2_in, g2_send, g2_recv, far)
    train_inv = lax.rsqrt(message[8:16] / K + 1e-06)
    val_inv = lax.rsqrt(message[16:24] / K + 1e-06)
    scores = message[:8] * train_inv * val_inv * (1.0 / K)
    for b in range(TRAIN_ROWS // 8):
        at = slice(b * 8, (b + 1) * 8)
        scores_ref[at, :] = scores[:, b * all_val : (b + 1) * all_val]
        scale = jnp.broadcast_to(train_inv[:, b * all_val : b * all_val + 1], (8, LANES))
        feat_ref[at, :] = trains[at] * scale

    for d in range(1, ny):
        train_copy(d, y0).wait_send()
        val_copy(d, y0).wait_send()

    def sent(i, carry):
        core_copy(i * 2).wait_send()
        core_copy(i * 2 + 1).wait_send()
        for d in range(1, NX):
            x_copy(i, d).wait_send()
        for d in range(1, ny):
            y_copy(i, d).wait_send()
        return carry

    lax.fori_loop(0, nz, sent, 0)
    lax.fori_loop(0, nz - 1, lambda i, c: (z_copy(i).wait_send(), c)[1], 0)
    for copy in copies1 + copies2:
        copy.wait_send()


def per_device(ny, par, train, val, m1, m2, rows, cols, off):
    nz = par // (NX * NC)
    local = train.shape[1]
    depth = local // ny
    all_rows = ny * (TRAIN_ROWS + VAL_ROWS)
    piece = TRAIN_ROWS + ny * VAL_ROWS
    tiles = nz * NX
    gen_first = 2 * ((tiles * 5 // 8) // 2)
    vmem = pl.BlockSpec(memory_space=pltpu.VMEM)
    f32, bf16 = jnp.float32, jnp.bfloat16
    dma = pltpu.SemaphoreType.DMA
    return pl.pallas_call(
        functools.partial(kernel, ny, nz, gen_first),
        out_shape=(
            jax.ShapeDtypeStruct((TRAIN_ROWS, LANES), f32),
            jax.ShapeDtypeStruct((TRAIN_ROWS, ny * VAL_ROWS), f32),
        ),
        in_specs=[pl.BlockSpec(memory_space=pl.ANY)] + [vmem] * 5 + [pl.BlockSpec(memory_space=pltpu.SMEM)],
        out_specs=(vmem, vmem),
        scratch_shapes=[
            pltpu.VMEM((depth, LANES), jnp.int32),
            pltpu.VMEM((ny, TRAIN_ROWS, depth), bf16),
            pltpu.VMEM((ny - 1, 2 * VAL_ROWS, depth // 2), bf16),
            pltpu.VMEM((ny, 2 * VAL_ROWS, depth // 2), bf16),
            pltpu.VMEM((depth // LANES, all_rows, LANES), bf16),
            pltpu.VMEM((tiles, depth, 2 * LANES), bf16),
            pltpu.VMEM((2 * nz, 2, all_rows, LANES), f32),
            pltpu.VMEM((2 * nz, 2, all_rows, LANES), f32),
            pltpu.VMEM((2 * nz, 2, all_rows, LANES), f32),
            pltpu.VMEM((nz, NX - 1, all_rows, LANES), bf16),
            pltpu.VMEM((nz, NX - 1, all_rows, LANES), bf16),
            pltpu.VMEM((all_rows, LANES), f32),
            pltpu.VMEM((nz, ny - 1, piece, LANES), bf16),
            pltpu.VMEM((nz, ny - 1, piece, LANES), bf16),
            pltpu.VMEM((nz, piece, LANES), f32),
            pltpu.VMEM((nz - 1, piece, LANES), f32),
            pltpu.VMEM((nz - 1, piece, LANES), f32),
            pltpu.VMEM((24, LANES), f32),
            pltpu.VMEM((NX * NC - 1, 24, LANES), f32),
            pltpu.VMEM((24, LANES), f32),
            pltpu.VMEM((nz - 1, 24, LANES), f32),
            dma((2, ny - 1)), dma((2, ny - 1)), dma,
            dma((2 * nz,)), dma((2 * nz,)),
            dma((nz, NX - 1)), dma((nz, NX - 1)),
            dma((nz, ny - 1)), dma((nz, ny - 1)),
            dma((nz - 1,)), dma((nz - 1,)),
            dma((NX * NC - 1,)), dma((NX * NC - 1,)),
            dma((nz - 1,)), dma((nz - 1,)),
        ],
        compiler_params=pltpu.CompilerParams(
            collective_id=0, has_side_effects=True, vmem_limit_bytes=60 << 20
        ),
        name="project",
    )(
        train, val, m1.reshape(1, local), m2.reshape(1, local),
        rows.reshape(local // LANES, LANES), cols.reshape(1, cols.shape[0]), off,
    )


def solution(mesh):
    in_specs = (P("ex", "par"), P("ex", "par"), P("par"), P("par"), P("par"), P(), P())
    out_specs = (P("ex", "par"), P("ex", None))
    body = functools.partial(per_device, mesh.shape["ex"], mesh.shape["par"])
    return jax.shard_map(body, mesh=mesh, in_specs=in_specs, out_specs=out_specs, check_vma=False)
```

```python
import functools
import math

import jax
import jax.numpy as jnp
from jax import lax
from jax.experimental import pallas as pl
from jax.experimental.pallas import tpu as pltpu
from jax.sharding import PartitionSpec as P

K = 8192
P_SIZE = 524288
MESH = pl.DeviceIdType.MESH
LANES = 128
NX = 4
NC = 2
TRAIN_ROWS = 32
VAL_ROWS = 8
SIGN_FACTOR = ((739982445 << 15) + 2**31) % 2**32 - 2**31
CORE_LAG, RELAY_LAG, X_LAG, Y_LAG = 1, 3, 6, 9


def make_entries(row_b, cols, offset, dest, depth, start):
    step = 128
    for first in range(0, depth, step):
        rows = row_b[first : first + step, :]
        for half, col in enumerate(cols):
            mixed = rows * col + offset
            mixed = mixed ^ (mixed >> 15)
            mixed = mixed * SIGN_FACTOR
            dest[first : first + step, pl.ds(pl.multiple_of(start + half * LANES, LANES), LANES)] = jnp.where(
                mixed < 0, jnp.bfloat16(1), jnp.bfloat16(-1)
            )


def kernel(
    ny, nz, gen_early, gen_first,
    train_ref, val_ref, m1_ref, m2_ref, rows_ref, cols_ref, off_ref,
    feat_ref, scores_ref,
    row_b, train_in, val_out, val_in, g_ref, tiles,
    core_out, core_in, own, r_out, r_in, x_out, x_in, x_sum, y_out, y_in, y_own, z_out, z_in, yz_out, yz_in,
    g1_out, g1_in, g2_out, g2_in,
    in_send, in_recv, in_local, core_send, core_recv, r_send, r_recv, x_send, x_recv, y_send, y_recv, z_send, z_recv, yz_send, yz_recv,
    g1_send, g1_recv, g2_send, g2_recv,
):
    y0 = lax.axis_index("ex")
    q0 = lax.axis_index("par")
    c0 = lax.rem(q0, NC)
    x0 = lax.rem(q0 // NC, NX)
    z0 = q0 // (NC * NX)
    depth = row_b.shape[0]
    all_train = ny * TRAIN_ROWS
    all_val = ny * VAL_ROWS
    all_rows = all_train + all_val
    piece = TRAIN_ROWS + all_val

    def par_of(z, x, c):
        return (z * NX + x) * NC + c

    peers = [(y0, par_of(z0, x0, 1 - c0))]
    peers += [(y0, par_of(z0, lax.rem(x0 + d, NX), c)) for d in range(1, NX) for c in (c0, 1 - c0)]
    peers += [(lax.rem(y0 + d, ny), q0) for d in range(1, ny)]
    peers += [(y0, par_of(lax.rem(z0 + d, nz), x0, c0)) for d in range(1, nz)]
    peers += [(lax.rem(y0 + d, ny), par_of(lax.rem(z0 + 1, nz), x0, c0)) for d in range(1, ny)]
    barrier = pltpu.get_barrier_semaphore()
    for peer in peers:
        pl.semaphore_signal(barrier, inc=1, device_id=peer, device_id_type=MESH)

    def remote(src, dst, send, recv, peer):
        return pltpu.make_async_remote_copy(
            src_ref=src, dst_ref=dst, send_sem=send, recv_sem=recv, device_id=peer, device_id_type=MESH
        )

    def train_copy(d, slot):
        e = lax.rem(y0 + d, ny)
        return remote(
            train_ref.at[:, pl.ds(pl.multiple_of(e * depth, LANES), depth)],
            train_in.at[slot], in_send.at[0, d - 1], in_recv.at[0, d - 1], (e, q0),
        )

    def val_copy(d, slot):
        e = lax.rem(y0 + d, ny)
        return remote(val_out.at[d - 1], val_in.at[slot], in_send.at[1, d - 1], in_recv.at[1, d - 1], (e, q0))

    groups = depth // LANES
    codes = rows_ref[pl.ds(pl.multiple_of(y0 * groups, groups), groups), :].T
    for j in range(groups):
        row_b[j * LANES : (j + 1) * LANES, :] = jnp.broadcast_to(codes[:, j : j + 1], (LANES, LANES))
    offset = off_ref[0]

    order = (2, 1, 3, 0)

    def z_distance(i):
        return nz // 2 + jnp.where(lax.rem(i, 2) == 0, i // 2, -((i + 1) // 2))

    def tile_features(t, step_in_chunk):
        z = lax.rem(z0 + z_distance(t), nz)
        x = lax.rem(x0 + step_in_chunk, NX)
        base = par_of(z, x, 0) * LANES
        mine = cols_ref[:, pl.ds(pl.multiple_of(base + c0 * LANES, LANES), LANES)]
        other = cols_ref[:, pl.ds(pl.multiple_of(base + (1 - c0) * LANES, LANES), LANES)]
        return mine, other

    def distance(k):
        return jnp.where(k == 0, 2, jnp.where(k == 1, 1, jnp.where(k == 2, 3, 0)))

    def generate(t):
        cols = tile_features(t // NX, distance(lax.rem(t, NX)))
        make_entries(row_b, cols, offset, tiles.at[t // 2], depth, lax.rem(t, 2) * (2 * LANES))

    half = depth // 2
    for d in range(ny):
        e = lax.rem(y0 + d, ny)
        upper = val_ref[:, pl.ds(pl.multiple_of(e * depth, LANES), half)].astype(jnp.float32)
        lower = val_ref[:, pl.ds(pl.multiple_of(e * depth + half, LANES), half)].astype(jnp.float32)
        stacked = jnp.concatenate([upper, lower], axis=0).astype(jnp.bfloat16)
        if d == 0:
            val_in[y0] = stacked
        else:
            val_out[d - 1] = stacked

    lax.fori_loop(0, gen_early, lambda t, c: (generate(t), c)[1], 0)
    pl.semaphore_wait(barrier, len(peers))
    for d in range(1, ny):
        train_copy(d, y0).start()
        val_copy(d, y0).start()
    local_copy = pltpu.make_async_copy(
        train_ref.at[:, pl.ds(pl.multiple_of(y0 * depth, LANES), depth)], train_in.at[y0], in_local
    )
    local_copy.start()

    lax.fori_loop(gen_early, gen_first, lambda t, c: (generate(t), c)[1], 0)

    local_copy.wait()
    for d in range(1, ny):
        source = lax.rem(y0 + ny - d, ny)
        train_copy(d, source).wait_recv()
        val_copy(d, source).wait_recv()

    def fill(j, carry):
        vals = [[], []]
        at = pl.ds(pl.multiple_of(j * LANES, LANES), LANES)
        for e in range(ny):
            both = val_in[e, :, at].astype(jnp.float32)
            vals[0].append(both[:VAL_ROWS])
            vals[1].append(both[VAL_ROWS:])
        for h in range(2):
            block = j + h * (groups // 2)
            here = pl.ds(pl.multiple_of(block * LANES, LANES), LANES)
            there = pl.ds(pl.multiple_of(y0 * depth + block * LANES, LANES), LANES)
            m1 = 0.9 * m1_ref[:, there]
            m2 = 0.999 * m2_ref[:, there]
            for e in range(ny):
                g = train_in[e, :, here].astype(jnp.float32)
                direction = (m1 + 0.1 * g) / (jnp.sqrt(m2 + 0.001 * g * g) + 1e-08)
                g_ref[block, e * TRAIN_ROWS : (e + 1) * TRAIN_ROWS, :] = direction.astype(jnp.bfloat16)
            g_ref[block, all_train:all_rows, :] = jnp.concatenate(vals[h], axis=0).astype(jnp.bfloat16)
        return carry

    lax.fori_loop(0, groups // 2, fill, 0)

    sibling = (y0, par_of(z0, x0, 1 - c0))

    def core_copy(i):
        return remote(core_out.at[i], core_in.at[i], core_send.at[i], core_recv.at[i], sibling)

    x_steps = (1, NX - 1)

    def x_peer(side):
        return (y0, par_of(z0, lax.rem(x0 + x_steps[side], NX), c0))

    def relay_copy(i, side):
        return remote(r_out.at[i, side], r_in.at[i, side], r_send.at[i, side], r_recv.at[i, side], x_peer(side))

    def x_copy(i, side):
        return remote(x_out.at[i, side], x_in.at[i, side], x_send.at[i, side], x_recv.at[i, side], x_peer(side))

    def y_copy(i, d):
        peer = (lax.rem(y0 + d, ny), q0)
        return remote(y_out.at[i, d - 1], y_in.at[i, d - 1], y_send.at[i, d - 1], y_recv.at[i, d - 1], peer)

    def z_copy(i):
        peer = (y0, par_of(lax.rem(z0 + z_distance(i), nz), x0, c0))
        return remote(z_out.at[i], z_in.at[i], z_send.at[i], z_recv.at[i], peer)

    def yz_copy(dy):
        peer = (lax.rem(y0 + dy, ny), par_of(lax.rem(z0 + nz - 1, nz), x0, c0))
        return remote(yz_out.at[dy], yz_in.at[dy], yz_send.at[dy], yz_recv.at[dy], peer)

    def multiply(i):
        lhs = jnp.concatenate([g_ref[b] for b in range(groups)], axis=1)
        for pair in range(2):
            part = jnp.dot(lhs, tiles[i * 2 + pair], preferred_element_type=jnp.float32)
            for k in range(2):
                at = 2 * k * LANES
                own[i, pair * 2 + k] = part[:, at : at + LANES]
                core_out[i, pair * 2 + k] = part[:, at + LANES : at + 2 * LANES]
        core_copy(i).start()

    upper_rows = all_rows // 2

    def piece_of(rows, dy):
        e = lax.rem(y0 + dy, ny)
        trains = rows[pl.ds(pl.multiple_of(e * TRAIN_ROWS, TRAIN_ROWS), TRAIN_ROWS), :]
        return jnp.concatenate([trains, rows[all_train:, :]], axis=0)

    def after_core(i):
        core_copy(i).wait_recv()
        for k in range(NX):
            total = own[i, k] + core_in[i, k]
            if order[k] == 2:
                r_out[i, 0] = total[:upper_rows].astype(jnp.bfloat16)
                r_out[i, 1] = total[upper_rows:].astype(jnp.bfloat16)
                relay_copy(i, 0).start()
                relay_copy(i, 1).start()
            else:
                own[i, k] = total

    def after_relay(i):
        for side in range(2):
            relay_copy(i, side).wait_recv()
            total = own[i, order.index(x_steps[side])]
            parts = [total[:upper_rows], total[upper_rows:]]
            parts[side] = parts[side] + r_in[i, side].astype(jnp.float32)
            x_out[i, side] = jnp.concatenate(parts, axis=0).astype(jnp.bfloat16)
            x_copy(i, side).start()

    def after_x(i):
        total = own[i, order.index(0)]
        for side in range(2):
            x_copy(i, side).wait_recv()
            total = total + x_in[i, side].astype(jnp.float32)
        x_sum[...] = total

        @pl.when(i != nz - 2)
        def _():
            for d in range(1, ny):
                y_out[i, d - 1] = piece_of(x_sum, d).astype(jnp.bfloat16)
                y_copy(i, d).start()
            y_own[i] = piece_of(x_sum, 0)

        @pl.when(i == nz - 2)
        def _():
            for dy in (2, 1, 3, 0):
                yz_out[dy] = piece_of(x_sum, dy).astype(jnp.bfloat16)
                yz_copy(dy).start()

    def y_total(i):
        total = y_own[i]
        for d in range(1, ny):
            y_copy(i, d).wait_recv()
            total = total + y_in[i, d - 1].astype(jnp.float32)
        return total

    def after_y(i):
        z_out[i] = y_total(i)
        z_copy(i).start()

    def stage(i, lag, work, count):
        @pl.when((i >= lag) & (i < lag + count))
        def _():
            work(i - lag)

    def passed_on(i):
        stage(i, CORE_LAG, after_core, nz)
        stage(i, Y_LAG, after_y, nz - 2)
        stage(i, X_LAG, after_x, nz)
        stage(i, RELAY_LAG, after_relay, nz)

    def with_gen(i, carry):
        for k in range(2):
            generate(gen_first + i * 2 + k)
        multiply(i)
        passed_on(i)
        return carry

    def without_gen(i, carry):
        multiply(i)
        passed_on(i)
        return carry

    def rest(i, carry):
        passed_on(i)
        return carry

    gen_steps = (nz * NX - gen_first) // 2
    lax.fori_loop(0, gen_steps, with_gen, 0)
    lax.fori_loop(gen_steps, nz, without_gen, 0)
    lax.fori_loop(nz, nz - 2 + Y_LAG, rest, 0)
    total = y_total(nz - 1)
    for i in range(nz - 2):
        z_copy(i).wait_recv()
        total = total + z_in[i]
    for dy in range(ny):
        yz_copy(dy).wait_recv()
        total = total + yz_in[dy].astype(jnp.float32)

    total = total * (1.0 / math.sqrt(P_SIZE))
    trains, vals = total[:TRAIN_ROWS], total[TRAIN_ROWS:]
    fold = LANES // all_val
    wide = jnp.concatenate([vals] * fold, axis=0)
    dims = (((1,), (1,)), ((), ()))
    inner = lax.dot_general(trains, wide, dims, precision=lax.Precision.HIGHEST, preferred_element_type=jnp.float32)
    val_sq = lax.dot_general(
        jnp.ones((8, LANES), jnp.float32), wide * wide, dims,
        precision=lax.Precision.HIGHEST, preferred_element_type=jnp.float32,
    )
    train_sq = jnp.broadcast_to(jnp.sum(trains * trains, axis=1, keepdims=True), (TRAIN_ROWS, LANES))
    block = lax.broadcasted_iota(jnp.int32, (8, LANES), 1) // all_val

    def packed(a):
        out = a[:8]
        for b in range(1, TRAIN_ROWS // 8):
            out = jnp.where(block == b, a[b * 8 : (b + 1) * 8], out)
        return out

    def share(message, out_ref, in_ref, send, recv, targets, meanwhile):
        out_ref[...] = message
        copies = [
            remote(out_ref, in_ref.at[n], send.at[n], recv.at[n], target) for n, target in enumerate(targets)
        ]
        for copy in copies:
            copy.start()
        meanwhile()
        for n, copy in enumerate(copies):
            copy.wait_recv()
            message = message + in_ref[n]
        return message, copies

    def all_sent():
        for d in range(1, ny):
            train_copy(d, y0).wait_send()
            val_copy(d, y0).wait_send()

        def sent(i, carry):
            core_copy(i).wait_send()
            for side in range(2):
                relay_copy(i, side).wait_send()
                x_copy(i, side).wait_send()
            return carry

        def yz_sent(i, carry):
            for d in range(1, ny):
                y_copy(i, d).wait_send()
            z_copy(i).wait_send()
            return carry

        lax.fori_loop(0, nz, sent, 0)
        lax.fori_loop(0, nz - 2, yz_sent, 0)
        for d in range(1, ny):
            y_copy(nz - 1, d).wait_send()
        for dy in range(ny):
            yz_copy(dy).wait_send()

    def turned(a, by):
        return jnp.concatenate([a[:, LANES - by :], a[:, : LANES - by]], axis=1)

    part = all_val // 2
    lower = lax.rem(lax.broadcasted_iota(jnp.int32, (8, LANES), 1), all_val) < part
    odd = lax.rem(block, 2) == 1
    squares = jnp.where(lower, packed(train_sq), jnp.where(odd, val_sq, turned(val_sq, part)))
    message = jnp.concatenate([packed(inner), squares], axis=0)
    near = [(y0, par_of(z0, lax.rem(x0 + d, NX), c)) for d in range(NX) for c in (c0, 1 - c0)][1:]
    message, copies1 = share(message, g1_out, g1_in, g1_send, g1_recv, near, all_sent)
    far = [(y0, par_of(lax.rem(z0 + d, nz), x0, c0)) for d in range(1, nz)]
    message, copies2 = share(message, g2_out, g2_in, g2_send, g2_recv, far, lambda: None)
    inverse = lax.rsqrt(message[8:] / K + 1e-06)
    before = turned(inverse, part)
    train_inv = jnp.where(lower, inverse, before)
    val_inv = jnp.where(
        odd, jnp.where(lower, before, inverse),
        jnp.where(lower, turned(inverse, LANES - part), turned(inverse, LANES - 2 * part)),
    )
    scores = message[:8] * train_inv * val_inv * (1.0 / K)
    for b in range(TRAIN_ROWS // 8):
        at = slice(b * 8, (b + 1) * 8)
        scores_ref[at, :] = scores[:, b * all_val : (b + 1) * all_val]
        scale = jnp.broadcast_to(train_inv[:, b * all_val : b * all_val + 1], (8, LANES))
        feat_ref[at, :] = trains[at] * scale

    for copy in copies1 + copies2:
        copy.wait_send()


def per_device(ny, par, train, val, m1, m2, rows, cols, off):
    nz = par // (NX * NC)
    local = train.shape[1]
    depth = local // ny
    all_rows = ny * (TRAIN_ROWS + VAL_ROWS)
    piece = TRAIN_ROWS + ny * VAL_ROWS
    tiles = nz * NX
    gen_early, gen_first = tiles // 4, 2 * (tiles * 13 // 32)
    vmem = pl.BlockSpec(memory_space=pltpu.VMEM)
    f32, bf16 = jnp.float32, jnp.bfloat16
    dma = pltpu.SemaphoreType.DMA
    return pl.pallas_call(
        functools.partial(kernel, ny, nz, gen_early, gen_first),
        out_shape=(
            jax.ShapeDtypeStruct((TRAIN_ROWS, LANES), f32),
            jax.ShapeDtypeStruct((TRAIN_ROWS, ny * VAL_ROWS), f32),
        ),
        in_specs=[pl.BlockSpec(memory_space=pl.ANY)] + [vmem] * 5 + [pl.BlockSpec(memory_space=pltpu.SMEM)],
        out_specs=(vmem, vmem),
        scratch_shapes=[
            pltpu.VMEM((depth, LANES), jnp.int32),
            pltpu.VMEM((ny, TRAIN_ROWS, depth), bf16),
            pltpu.VMEM((ny - 1, 2 * VAL_ROWS, depth // 2), bf16),
            pltpu.VMEM((ny, 2 * VAL_ROWS, depth // 2), bf16),
            pltpu.VMEM((depth // LANES, all_rows, LANES), bf16),
            pltpu.VMEM((tiles // 2, depth, 4 * LANES), bf16),
            pltpu.VMEM((nz, NX, all_rows, LANES), f32),
            pltpu.VMEM((nz, NX, all_rows, LANES), f32),
            pltpu.VMEM((nz, NX, all_rows, LANES), f32),
            pltpu.VMEM((nz, 2, all_rows // 2, LANES), bf16),
            pltpu.VMEM((nz, 2, all_rows // 2, LANES), bf16),
            pltpu.VMEM((nz, 2, all_rows, LANES), bf16),
            pltpu.VMEM((nz, 2, all_rows, LANES), bf16),
            pltpu.VMEM((all_rows, LANES), f32),
            pltpu.VMEM((nz, ny - 1, piece, LANES), bf16),
            pltpu.VMEM((nz, ny - 1, piece, LANES), bf16),
            pltpu.VMEM((nz, piece, LANES), f32),
            pltpu.VMEM((nz - 2, piece, LANES), f32),
            pltpu.VMEM((nz - 2, piece, LANES), f32),
            pltpu.VMEM((ny, piece, LANES), bf16),
            pltpu.VMEM((ny, piece, LANES), bf16),
            pltpu.VMEM((16, LANES), f32),
            pltpu.VMEM((NX * NC - 1, 16, LANES), f32),
            pltpu.VMEM((16, LANES), f32),
            pltpu.VMEM((nz - 1, 16, LANES), f32),
            dma((2, ny - 1)), dma((2, ny - 1)), dma,
            dma((nz,)), dma((nz,)),
            dma((nz, 2)), dma((nz, 2)),
            dma((nz, 2)), dma((nz, 2)),
            dma((nz, ny - 1)), dma((nz, ny - 1)),
            dma((nz - 2,)), dma((nz - 2,)),
            dma((ny,)), dma((ny,)),
            dma((NX * NC - 1,)), dma((NX * NC - 1,)),
            dma((nz - 1,)), dma((nz - 1,)),
        ],
        compiler_params=pltpu.CompilerParams(
            collective_id=0, has_side_effects=True, vmem_limit_bytes=60 << 20
        ),
        name="project",
    )(
        train, val, m1.reshape(1, local), m2.reshape(1, local),
        rows.reshape(local // LANES, LANES), cols.reshape(1, cols.shape[0]), off,
    )


def solution(mesh):
    in_specs = (P("ex", "par"), P("ex", "par"), P("par"), P("par"), P("par"), P(), P())
    out_specs = (P("ex", "par"), P("ex", None))
    body = functools.partial(per_device, mesh.shape["ex"], mesh.shape["par"])
    return jax.shard_map(body, mesh=mesh, in_specs=in_specs, out_specs=out_specs, check_vma=False)
```

```python
import functools
import math

import jax
import jax.numpy as jnp
from jax import lax
from jax.experimental import pallas as pl
from jax.experimental.pallas import tpu as pltpu
from jax.sharding import PartitionSpec as P

K = 8192
P_SIZE = 524288
MESH = pl.DeviceIdType.MESH
LANES = 128
NX = 4
NC = 2
TRAIN_ROWS = 32
VAL_ROWS = 8
SIGN_FACTOR = ((739982445 << 15) + 2**31) % 2**32 - 2**31
CORE_LAG, RELAY_LAG, X_LAG, Y_LAG = 1, 3, 6, 9


def make_entries(row_b, cols, offset, dest, depth, start):
    step = 128
    for first in range(0, depth, step):
        rows = row_b[first : first + step, :]
        for half, col in enumerate(cols):
            mixed = rows * col + offset
            mixed = mixed ^ (mixed >> 15)
            mixed = mixed * SIGN_FACTOR
            dest[first : first + step, pl.ds(pl.multiple_of(start + half * LANES, LANES), LANES)] = jnp.where(
                mixed < 0, jnp.bfloat16(1), jnp.bfloat16(-1)
            )


def turned(a, by):
    return jnp.concatenate([a[:, LANES - by :], a[:, : LANES - by]], axis=1)


def lane_masks(width):
    lane = lax.broadcasted_iota(jnp.int32, (8, LANES), 1)
    return lax.rem(lane, width) < width // 2, lax.rem(lane // width, 2) == 1


def finish(all_val, raw_ref, message_ref, feat_ref, scores_ref):
    part = all_val // 2
    lower, odd = lane_masks(all_val)
    inverse = lax.rsqrt(message_ref[8:] / K + 1e-06)
    before = turned(inverse, part)
    train_inv = jnp.where(lower, inverse, before)
    val_inv = jnp.where(
        odd, jnp.where(lower, before, inverse),
        jnp.where(lower, turned(inverse, LANES - part), turned(inverse, LANES - 2 * part)),
    )
    scores = message_ref[:8] * train_inv * val_inv * (1.0 / K)
    for b in range(TRAIN_ROWS // 8):
        at = slice(b * 8, (b + 1) * 8)
        scores_ref[at, :] = scores[:, b * all_val : (b + 1) * all_val]
        scale = jnp.broadcast_to(train_inv[:, b * all_val : b * all_val + 1], (8, LANES))
        feat_ref[at, :] = raw_ref[at, :] * scale


def kernel(
    ny, nz, gen_early, gen_first,
    train_ref, val_ref, m1_ref, m2_ref, rows_ref, cols_ref, off_ref,
    raw_ref, message_ref,
    row_b, train_in, val_out, val_in, g_ref, tiles, late_tiles,
    core_out, core_in, own, r_out, r_in, x_out, x_in, x_sum, y_out, y_in, y_own, z_out, z_in, yz_out, yz_in,
    g1_out, g1_in, g2_out, g2_in,
    in_send, in_recv, in_local, core_send, core_recv, r_send, r_recv, x_send, x_recv, y_send, y_recv, z_send, z_recv, yz_send, yz_recv,
    g1_send, g1_recv, g2_send, g2_recv,
):
    y0 = lax.axis_index("ex")
    q0 = lax.axis_index("par")
    c0 = lax.rem(q0, NC)
    x0 = lax.rem(q0 // NC, NX)
    z0 = q0 // (NC * NX)
    depth = row_b.shape[0]
    all_train = ny * TRAIN_ROWS
    all_val = ny * VAL_ROWS
    all_rows = all_train + all_val
    piece = TRAIN_ROWS + all_val

    def par_of(z, x, c):
        return (z * NX + x) * NC + c

    peers = [(y0, par_of(z0, x0, 1 - c0))]
    peers += [(y0, par_of(z0, lax.rem(x0 + d, NX), c)) for d in range(1, NX) for c in (c0, 1 - c0)]
    peers += [(lax.rem(y0 + d, ny), q0) for d in range(1, ny)]
    peers += [(y0, par_of(lax.rem(z0 + d, nz), x0, c0)) for d in range(1, nz)]
    peers += [(lax.rem(y0 + d, ny), par_of(lax.rem(z0 + 1, nz), x0, c0)) for d in range(1, ny)]
    barrier = pltpu.get_barrier_semaphore()
    for peer in peers:
        pl.semaphore_signal(barrier, inc=1, device_id=peer, device_id_type=MESH)

    def remote(src, dst, send, recv, peer):
        return pltpu.make_async_remote_copy(
            src_ref=src, dst_ref=dst, send_sem=send, recv_sem=recv, device_id=peer, device_id_type=MESH
        )

    def train_copy(d, slot):
        e = lax.rem(y0 + d, ny)
        return remote(
            train_ref.at[:, pl.ds(pl.multiple_of(e * depth, LANES), depth)],
            train_in.at[slot], in_send.at[0, d - 1], in_recv.at[0, d - 1], (e, q0),
        )

    def val_copy(d, slot):
        e = lax.rem(y0 + d, ny)
        return remote(val_out.at[d - 1], val_in.at[slot], in_send.at[1, d - 1], in_recv.at[1, d - 1], (e, q0))

    groups = depth // LANES
    codes = rows_ref[pl.ds(pl.multiple_of(y0 * groups, groups), groups), :].T
    for j in range(groups):
        row_b[j * LANES : (j + 1) * LANES, :] = jnp.broadcast_to(codes[:, j : j + 1], (LANES, LANES))
    offset = off_ref[0]

    order = (2, 1, 3, 0)

    def z_distance(i):
        return nz // 2 + jnp.where(lax.rem(i, 2) == 0, i // 2, -((i + 1) // 2))

    def tile_features(t, step_in_chunk):
        z = lax.rem(z0 + z_distance(t), nz)
        x = lax.rem(x0 + step_in_chunk, NX)
        base = par_of(z, x, 0) * LANES
        mine = cols_ref[:, pl.ds(pl.multiple_of(base + c0 * LANES, LANES), LANES)]
        other = cols_ref[:, pl.ds(pl.multiple_of(base + (1 - c0) * LANES, LANES), LANES)]
        return mine, other

    def distance(k):
        return jnp.where(k == 0, 2, jnp.where(k == 1, 1, jnp.where(k == 2, 3, 0)))

    def generate(t, dest, at):
        cols = tile_features(t // NX, distance(lax.rem(t, NX)))
        make_entries(row_b, cols, offset, dest.at[at // 2], depth, lax.rem(at, 2) * (2 * LANES))

    half = depth // 2
    for d in range(ny):
        e = lax.rem(y0 + d, ny)
        upper = val_ref[:, pl.ds(pl.multiple_of(e * depth, LANES), half)].astype(jnp.float32)
        lower = val_ref[:, pl.ds(pl.multiple_of(e * depth + half, LANES), half)].astype(jnp.float32)
        stacked = jnp.concatenate([upper, lower], axis=0).astype(jnp.bfloat16)
        if d == 0:
            val_in[y0] = stacked
        else:
            val_out[d - 1] = stacked

    lax.fori_loop(0, gen_early, lambda t, c: (generate(t, tiles, t), c)[1], 0)
    pl.semaphore_wait(barrier, len(peers))
    for d in sorted(range(1, ny), key=lambda d: -min(d, ny - d)):
        train_copy(d, y0).start()
        val_copy(d, y0).start()
    local_copy = pltpu.make_async_copy(
        train_ref.at[:, pl.ds(pl.multiple_of(y0 * depth, LANES), depth)], train_in.at[y0], in_local
    )
    local_copy.start()

    lax.fori_loop(gen_early, gen_first, lambda t, c: (generate(t, tiles, t), c)[1], 0)

    local_copy.wait()
    for d in range(1, ny):
        source = lax.rem(y0 + ny - d, ny)
        train_copy(d, source).wait_recv()
        val_copy(d, source).wait_recv()

    def fill(j, carry):
        vals = [[], []]
        at = pl.ds(pl.multiple_of(j * LANES, LANES), LANES)
        for e in range(ny):
            both = val_in[e, :, at].astype(jnp.float32)
            vals[0].append(both[:VAL_ROWS])
            vals[1].append(both[VAL_ROWS:])
        for h in range(2):
            block = j + h * (groups // 2)
            here = pl.ds(pl.multiple_of(block * LANES, LANES), LANES)
            there = pl.ds(pl.multiple_of(y0 * depth + block * LANES, LANES), LANES)
            m1 = 0.9 * m1_ref[:, there]
            m2 = 0.999 * m2_ref[:, there]
            for e in range(ny):
                g = train_in[e, :, here].astype(jnp.float32)
                direction = (m1 + 0.1 * g) / (jnp.sqrt(m2 + 0.001 * g * g) + 1e-08)
                g_ref[block, e * TRAIN_ROWS : (e + 1) * TRAIN_ROWS, :] = direction.astype(jnp.bfloat16)
            g_ref[block, all_train:all_rows, :] = jnp.concatenate(vals[h], axis=0).astype(jnp.bfloat16)
        return carry

    lax.fori_loop(0, groups // 2, fill, 0)

    sibling = (y0, par_of(z0, x0, 1 - c0))

    def core_copy(i):
        return remote(core_out.at[i], core_in.at[i], core_send.at[i], core_recv.at[i], sibling)

    x_steps = (1, NX - 1)

    def x_peer(side):
        return (y0, par_of(z0, lax.rem(x0 + x_steps[side], NX), c0))

    def relay_copy(i, side):
        return remote(r_out.at[i, side], r_in.at[i, side], r_send.at[i, side], r_recv.at[i, side], x_peer(side))

    def x_copy(i, side):
        return remote(x_out.at[i, side], x_in.at[i, side], x_send.at[i, side], x_recv.at[i, side], x_peer(side))

    def y_copy(i, d):
        peer = (lax.rem(y0 + d, ny), q0)
        return remote(y_out.at[i, d - 1], y_in.at[i, d - 1], y_send.at[i, d - 1], y_recv.at[i, d - 1], peer)

    def z_copy(i):
        peer = (y0, par_of(lax.rem(z0 + z_distance(i), nz), x0, c0))
        return remote(z_out.at[i], z_in.at[i], z_send.at[i], z_recv.at[i], peer)

    def yz_copy(dy):
        peer = (lax.rem(y0 + dy, ny), par_of(lax.rem(z0 + nz - 1, nz), x0, c0))
        return remote(yz_out.at[dy], yz_in.at[dy], yz_send.at[dy], yz_recv.at[dy], peer)

    def multiply(i, source):
        lhs = jnp.concatenate([g_ref[b] for b in range(groups)], axis=1)
        for pair in range(2):
            part = jnp.dot(lhs, source(pair), preferred_element_type=jnp.float32)
            for k in range(2):
                at = 2 * k * LANES
                own[i, pair * 2 + k] = part[:, at : at + LANES]
                core_out[i, pair * 2 + k] = part[:, at + LANES : at + 2 * LANES]
        core_copy(i).start()

    upper_rows = all_rows // 2

    def piece_of(rows, dy):
        e = lax.rem(y0 + dy, ny)
        trains = rows[pl.ds(pl.multiple_of(e * TRAIN_ROWS, TRAIN_ROWS), TRAIN_ROWS), :]
        return jnp.concatenate([trains, rows[all_train:, :]], axis=0)

    def after_core(i):
        core_copy(i).wait_recv()
        for k in range(NX):
            total = own[i, k] + core_in[i, k]
            if order[k] == 2:
                r_out[i, 0] = total[:upper_rows].astype(jnp.bfloat16)
                r_out[i, 1] = total[upper_rows:].astype(jnp.bfloat16)
                relay_copy(i, 0).start()
                relay_copy(i, 1).start()
            else:
                own[i, k] = total

    def after_relay(i):
        for side in range(2):
            relay_copy(i, side).wait_recv()
            total = own[i, order.index(x_steps[side])]
            parts = [total[:upper_rows], total[upper_rows:]]
            parts[side] = parts[side] + r_in[i, side].astype(jnp.float32)
            x_out[i, side] = jnp.concatenate(parts, axis=0).astype(jnp.bfloat16)
            x_copy(i, side).start()

    def after_x(i):
        total = own[i, order.index(0)]
        for side in range(2):
            x_copy(i, side).wait_recv()
            total = total + x_in[i, side].astype(jnp.float32)
        x_sum[...] = total

        @pl.when(i != nz - 2)
        def _():
            for d in range(1, ny):
                y_out[i, d - 1] = piece_of(x_sum, d).astype(jnp.bfloat16)
                y_copy(i, d).start()
            y_own[i] = piece_of(x_sum, 0)

        @pl.when(i == nz - 2)
        def _():
            for dy in (2, 1, 3, 0):
                yz_out[dy] = piece_of(x_sum, dy).astype(jnp.bfloat16)
                yz_copy(dy).start()

    def y_total(i):
        total = y_own[i]
        for d in range(1, ny):
            y_copy(i, d).wait_recv()
            total = total + y_in[i, d - 1].astype(jnp.float32)
        return total

    def after_y(i):
        z_out[i] = y_total(i)
        z_copy(i).start()

    def stage(i, lag, work, count):
        @pl.when((i >= lag) & (i < lag + count))
        def _():
            work(i - lag)

    def passed_on(i):
        stage(i, CORE_LAG, after_core, nz)
        stage(i, RELAY_LAG, after_relay, nz)
        stage(i, Y_LAG, after_y, nz - 2)
        stage(i, X_LAG, after_x, nz)

    mix_from = 0

    def with_gen(i, carry):
        for k in range(2):
            generate(gen_first + (i - mix_from) * 2 + k, late_tiles, (i - mix_from) * 2 + k)
        multiply(i, lambda pair: tiles[i * 2 + pair])
        passed_on(i)
        return carry

    def without_gen(i, carry):
        multiply(i, lambda pair: tiles[i * 2 + pair])
        passed_on(i)
        return carry

    def rest(i, carry):
        passed_on(i)
        return carry

    gen_steps = (nz * NX - gen_first) // 2
    lax.fori_loop(mix_from, mix_from + gen_steps, with_gen, 0)
    lax.fori_loop(mix_from + gen_steps, nz - 2, without_gen, 0)
    for i in (nz - 2, nz - 1):
        multiply(i, lambda pair: late_tiles[(i - nz + 2) * 2 + pair])
        passed_on(jnp.int32(i))
    lax.fori_loop(nz, nz - 2 + Y_LAG, rest, 0)
    total = y_total(nz - 1)
    for i in range(nz - 2):
        z_copy(i).wait_recv()
        total = total + z_in[i]
    for dy in range(ny):
        yz_copy(dy).wait_recv()
        total = total + yz_in[dy].astype(jnp.float32)

    total = total * (1.0 / math.sqrt(P_SIZE))
    trains, vals = total[:TRAIN_ROWS], total[TRAIN_ROWS:]
    fold = LANES // all_val
    wide = jnp.concatenate([vals] * fold, axis=0)
    dims = (((1,), (1,)), ((), ()))
    inner = lax.dot_general(trains, wide, dims, precision=lax.Precision.HIGHEST, preferred_element_type=jnp.float32)
    val_sq = lax.dot_general(
        jnp.ones((8, LANES), jnp.float32), wide * wide, dims,
        precision=lax.Precision.HIGHEST, preferred_element_type=jnp.float32,
    )
    train_sq = jnp.broadcast_to(jnp.sum(trains * trains, axis=1, keepdims=True), (TRAIN_ROWS, LANES))
    block = lax.broadcasted_iota(jnp.int32, (8, LANES), 1) // all_val

    def packed(a):
        out = a[:8]
        for b in range(1, TRAIN_ROWS // 8):
            out = jnp.where(block == b, a[b * 8 : (b + 1) * 8], out)
        return out

    def share(message, out_ref, in_ref, send, recv, targets, meanwhile):
        out_ref[...] = message
        copies = [
            remote(out_ref, in_ref.at[n], send.at[n], recv.at[n], target) for n, target in enumerate(targets)
        ]
        for copy in copies:
            copy.start()
        meanwhile()
        for n, copy in enumerate(copies):
            copy.wait_recv()
            message = message + in_ref[n]
        return message, copies

    def all_sent():
        for d in range(1, ny):
            train_copy(d, y0).wait_send()
            val_copy(d, y0).wait_send()

        def sent(i, carry):
            core_copy(i).wait_send()
            for side in range(2):
                relay_copy(i, side).wait_send()
                x_copy(i, side).wait_send()
            return carry

        def yz_sent(i, carry):
            for d in range(1, ny):
                y_copy(i, d).wait_send()
            z_copy(i).wait_send()
            return carry

        lax.fori_loop(0, nz, sent, 0)
        lax.fori_loop(0, nz - 2, yz_sent, 0)
        for d in range(1, ny):
            y_copy(nz - 1, d).wait_send()
        for dy in range(ny):
            yz_copy(dy).wait_send()

    part = all_val // 2
    lower, odd = lane_masks(all_val)
    squares = jnp.where(lower, packed(train_sq), jnp.where(odd, val_sq, turned(val_sq, part)))
    message = jnp.concatenate([packed(inner), squares], axis=0)
    near = [(y0, par_of(z0, lax.rem(x0 + d, NX), c)) for d in range(NX) for c in (c0, 1 - c0)][1:]
    message, copies1 = share(message, g1_out, g1_in, g1_send, g1_recv, near, all_sent)
    far = [(y0, par_of(lax.rem(z0 + d, nz), x0, c0)) for d in range(1, nz)]
    message, copies2 = share(message, g2_out, g2_in, g2_send, g2_recv, far, lambda: None)
    raw_ref[...] = trains
    message_ref[...] = message
    for copy in copies1 + copies2:
        copy.wait_send()


def per_device(ny, par, train, val, m1, m2, rows, cols, off):
    nz = par // (NX * NC)
    local = train.shape[1]
    depth = local // ny
    all_rows = ny * (TRAIN_ROWS + VAL_ROWS)
    piece = TRAIN_ROWS + ny * VAL_ROWS
    tiles = nz * NX
    gen_early, gen_first = 6, tiles - 8
    vmem = pl.BlockSpec(memory_space=pltpu.VMEM)
    f32, bf16 = jnp.float32, jnp.bfloat16
    dma = pltpu.SemaphoreType.DMA
    raw, message = pl.pallas_call(
        functools.partial(kernel, ny, nz, gen_early, gen_first),
        out_shape=(
            jax.ShapeDtypeStruct((TRAIN_ROWS, LANES), f32),
            jax.ShapeDtypeStruct((16, LANES), f32),
        ),
        in_specs=[pl.BlockSpec(memory_space=pl.ANY)] + [vmem] * 5 + [pl.BlockSpec(memory_space=pltpu.SMEM)],
        out_specs=(vmem, vmem),
        scratch_shapes=[
            pltpu.VMEM((depth, LANES), jnp.int32),
            pltpu.VMEM((ny, TRAIN_ROWS, depth), bf16),
            pltpu.VMEM((ny - 1, 2 * VAL_ROWS, depth // 2), bf16),
            pltpu.VMEM((ny, 2 * VAL_ROWS, depth // 2), bf16),
            pltpu.VMEM((depth // LANES, all_rows, LANES), bf16),
            pltpu.VMEM((tiles // 2 - 4, depth, 4 * LANES), bf16),
            pltpu.VMEM((4, depth, 4 * LANES), bf16),
            pltpu.VMEM((nz, NX, all_rows, LANES), f32),
            pltpu.VMEM((nz, NX, all_rows, LANES), f32),
            pltpu.VMEM((nz, NX, all_rows, LANES), f32),
            pltpu.VMEM((nz, 2, all_rows // 2, LANES), bf16),
            pltpu.VMEM((nz, 2, all_rows // 2, LANES), bf16),
            pltpu.VMEM((nz, 2, all_rows, LANES), bf16),
            pltpu.VMEM((nz, 2, all_rows, LANES), bf16),
            pltpu.VMEM((all_rows, LANES), f32),
            pltpu.VMEM((nz, ny - 1, piece, LANES), bf16),
            pltpu.VMEM((nz, ny - 1, piece, LANES), bf16),
            pltpu.VMEM((nz, piece, LANES), f32),
            pltpu.VMEM((nz - 2, piece, LANES), f32),
            pltpu.VMEM((nz - 2, piece, LANES), f32),
            pltpu.VMEM((ny, piece, LANES), bf16),
            pltpu.VMEM((ny, piece, LANES), bf16),
            pltpu.VMEM((16, LANES), f32),
            pltpu.VMEM((NX * NC - 1, 16, LANES), f32),
            pltpu.VMEM((16, LANES), f32),
            pltpu.VMEM((nz - 1, 16, LANES), f32),
            dma((2, ny - 1)), dma((2, ny - 1)), dma,
            dma((nz,)), dma((nz,)),
            dma((nz, 2)), dma((nz, 2)),
            dma((nz, 2)), dma((nz, 2)),
            dma((nz, ny - 1)), dma((nz, ny - 1)),
            dma((nz - 2,)), dma((nz - 2,)),
            dma((ny,)), dma((ny,)),
            dma((NX * NC - 1,)), dma((NX * NC - 1,)),
            dma((nz - 1,)), dma((nz - 1,)),
        ],
        compiler_params=pltpu.CompilerParams(
            collective_id=0, has_side_effects=True, vmem_limit_bytes=60 << 20
        ),
        name="project",
    )(
        train, val, m1.reshape(1, local), m2.reshape(1, local),
        rows.reshape(local // LANES, LANES), cols.reshape(1, cols.shape[0]), off,
    )
    return pl.pallas_call(
        functools.partial(finish, ny * VAL_ROWS),
        out_shape=(
            jax.ShapeDtypeStruct((TRAIN_ROWS, LANES), f32),
            jax.ShapeDtypeStruct((TRAIN_ROWS, ny * VAL_ROWS), f32),
        ),
        in_specs=[vmem, vmem],
        out_specs=(vmem, vmem),
        name="finish",
    )(raw, message)


def solution(mesh):
    in_specs = (P("ex", "par"), P("ex", "par"), P("par"), P("par"), P("par"), P(), P())
    out_specs = (P("ex", "par"), P("ex", None))
    body = functools.partial(per_device, mesh.shape["ex"], mesh.shape["par"])
    return jax.shard_map(body, mesh=mesh, in_specs=in_specs, out_specs=out_specs, check_vma=False)
```

```python
import functools
import math

import jax
import jax.numpy as jnp
from jax import lax
from jax.experimental import pallas as pl
from jax.experimental.pallas import tpu as pltpu
from jax.sharding import PartitionSpec as P

K = 8192
P_SIZE = 524288
MESH = pl.DeviceIdType.MESH
LANES = 128
NX = 4
NC = 2
TRAIN_ROWS = 32
VAL_ROWS = 8
SIGN_FACTOR = ((739982445 << 15) + 2**31) % 2**32 - 2**31
CORE_LAG, RELAY_LAG, X_LAG, Y_LAG = 1, 3, 6, 9


def make_entries(row_b, cols, offset, dest, depth, start):
    step = 128
    for first in range(0, depth, step):
        rows = row_b[first : first + step, :]
        for half, col in enumerate(cols):
            mixed = rows * col + offset
            mixed = mixed ^ (mixed >> 15)
            mixed = mixed * SIGN_FACTOR
            dest[first : first + step, pl.ds(pl.multiple_of(start + half * LANES, LANES), LANES)] = jnp.where(
                mixed < 0, jnp.bfloat16(1), jnp.bfloat16(-1)
            )


def turned(a, by):
    return jnp.concatenate([a[:, LANES - by :], a[:, : LANES - by]], axis=1)


def lane_masks(width):
    lane = lax.broadcasted_iota(jnp.int32, (8, LANES), 1)
    return lax.rem(lane, width) < width // 2, lax.rem(lane // width, 2) == 1


def finish(all_val, raw_ref, message_ref, feat_ref, scores_ref):
    part = all_val // 2
    lower, odd = lane_masks(all_val)
    inverse = lax.rsqrt(message_ref[8:] / K + 1e-06)
    before = turned(inverse, part)
    train_inv = jnp.where(lower, inverse, before)
    val_inv = jnp.where(
        odd, jnp.where(lower, before, inverse),
        jnp.where(lower, turned(inverse, LANES - part), turned(inverse, LANES - 2 * part)),
    )
    scores = message_ref[:8] * train_inv * val_inv * (1.0 / K)
    for b in range(TRAIN_ROWS // 8):
        at = slice(b * 8, (b + 1) * 8)
        scores_ref[at, :] = scores[:, b * all_val : (b + 1) * all_val]
        scale = jnp.broadcast_to(train_inv[:, b * all_val : b * all_val + 1], (8, LANES))
        feat_ref[at, :] = raw_ref[at, :] * scale


def kernel(
    ny, nz, gen_early, gen_first,
    train_ref, val_ref, m1_ref, m2_ref, rows_ref, cols_ref, off_ref,
    raw_ref, message_ref,
    row_b, train_in, val_out, val_in, g_ref, tiles, late_tiles,
    core_out, core_in, own, r_out, r_in, x_out, x_in, x_sum, y_out, y_in, y_own, z_out, z_in, yz_out, yz_in,
    g1_out, g1_in, g2_out, g2_in,
    in_send, in_recv, in_local, core_send, core_recv, r_send, r_recv, x_send, x_recv, y_send, y_recv, z_send, z_recv, yz_send, yz_recv,
    g1_send, g1_recv, g2_send, g2_recv,
):
    y0 = lax.axis_index("ex")
    q0 = lax.axis_index("par")
    c0 = lax.rem(q0, NC)
    x0 = lax.rem(q0 // NC, NX)
    z0 = q0 // (NC * NX)
    depth = row_b.shape[0]
    all_train = ny * TRAIN_ROWS
    all_val = ny * VAL_ROWS
    all_rows = all_train + all_val
    piece = TRAIN_ROWS + all_val

    def par_of(z, x, c):
        return (z * NX + x) * NC + c

    peers = [(y0, par_of(z0, x0, 1 - c0))]
    peers += [(y0, par_of(z0, lax.rem(x0 + d, NX), c)) for d in range(1, NX) for c in (c0, 1 - c0)]
    peers += [(lax.rem(y0 + d, ny), q0) for d in range(1, ny)]
    peers += [(y0, par_of(lax.rem(z0 + d, nz), x0, c0)) for d in range(1, nz)]
    peers += [(lax.rem(y0 + d, ny), par_of(lax.rem(z0 + 1, nz), x0, c0)) for d in range(1, ny)]
    barrier = pltpu.get_barrier_semaphore()
    for peer in peers:
        pl.semaphore_signal(barrier, inc=1, device_id=peer, device_id_type=MESH)

    def remote(src, dst, send, recv, peer):
        return pltpu.make_async_remote_copy(
            src_ref=src, dst_ref=dst, send_sem=send, recv_sem=recv, device_id=peer, device_id_type=MESH
        )

    def train_copy(d, slot):
        e = lax.rem(y0 + d, ny)
        return remote(
            train_ref.at[:, pl.ds(pl.multiple_of(e * depth, LANES), depth)],
            train_in.at[slot], in_send.at[0, d - 1], in_recv.at[0, d - 1], (e, q0),
        )

    def val_copy(d, slot):
        e = lax.rem(y0 + d, ny)
        return remote(val_out.at[d - 1], val_in.at[slot], in_send.at[1, d - 1], in_recv.at[1, d - 1], (e, q0))

    groups = depth // LANES
    codes = rows_ref[pl.ds(pl.multiple_of(y0 * groups, groups), groups), :].T
    for j in range(groups):
        row_b[j * LANES : (j + 1) * LANES, :] = jnp.broadcast_to(codes[:, j : j + 1], (LANES, LANES))
    offset = off_ref[0]

    order = (2, 1, 3, 0)

    def z_distance(i):
        return nz // 2 + jnp.where(lax.rem(i, 2) == 0, i // 2, -((i + 1) // 2))

    def tile_features(t, step_in_chunk):
        z = lax.rem(z0 + z_distance(t), nz)
        x = lax.rem(x0 + step_in_chunk, NX)
        base = par_of(z, x, 0) * LANES
        mine = cols_ref[:, pl.ds(pl.multiple_of(base + c0 * LANES, LANES), LANES)]
        other = cols_ref[:, pl.ds(pl.multiple_of(base + (1 - c0) * LANES, LANES), LANES)]
        return mine, other

    def distance(k):
        return jnp.where(k == 0, 2, jnp.where(k == 1, 1, jnp.where(k == 2, 3, 0)))

    def generate(t, dest, at):
        cols = tile_features(t // NX, distance(lax.rem(t, NX)))
        make_entries(row_b, cols, offset, dest.at[at // 2], depth, lax.rem(at, 2) * (2 * LANES))

    half = depth // 2
    for d in range(ny):
        e = lax.rem(y0 + d, ny)
        upper = val_ref[:, pl.ds(pl.multiple_of(e * depth, LANES), half)].astype(jnp.float32)
        lower = val_ref[:, pl.ds(pl.multiple_of(e * depth + half, LANES), half)].astype(jnp.float32)
        stacked = jnp.concatenate([upper, lower], axis=0).astype(jnp.bfloat16)
        if d == 0:
            val_in[y0] = stacked
        else:
            val_out[d - 1] = stacked

    lax.fori_loop(0, gen_early, lambda t, c: (generate(t, tiles, t), c)[1], 0)
    pl.semaphore_wait(barrier, len(peers))
    for d in sorted(range(1, ny), key=lambda d: -min(d, ny - d)):
        train_copy(d, y0).start()
        val_copy(d, y0).start()
    local_copy = pltpu.make_async_copy(
        train_ref.at[:, pl.ds(pl.multiple_of(y0 * depth, LANES), depth)], train_in.at[y0], in_local
    )
    local_copy.start()

    lax.fori_loop(gen_early, gen_first, lambda t, c: (generate(t, tiles, t), c)[1], 0)

    local_copy.wait()
    for d in range(1, ny):
        source = lax.rem(y0 + ny - d, ny)
        train_copy(d, source).wait_recv()
        val_copy(d, source).wait_recv()

    def fill(j, carry):
        vals = [[], []]
        at = pl.ds(pl.multiple_of(j * LANES, LANES), LANES)
        for e in range(ny):
            both = val_in[e, :, at].astype(jnp.float32)
            vals[0].append(both[:VAL_ROWS])
            vals[1].append(both[VAL_ROWS:])
        for h in range(2):
            block = j + h * (groups // 2)
            here = pl.ds(pl.multiple_of(block * LANES, LANES), LANES)
            there = pl.ds(pl.multiple_of(y0 * depth + block * LANES, LANES), LANES)
            m1 = 0.9 * m1_ref[:, there]
            m2 = 0.999 * m2_ref[:, there]
            for e in range(ny):
                g = train_in[e, :, here].astype(jnp.float32)
                direction = (m1 + 0.1 * g) / (jnp.sqrt(m2 + 0.001 * g * g) + 1e-08)
                g_ref[block, e * TRAIN_ROWS : (e + 1) * TRAIN_ROWS, :] = direction.astype(jnp.bfloat16)
            g_ref[block, all_train:all_rows, :] = jnp.concatenate(vals[h], axis=0).astype(jnp.bfloat16)
        return carry

    lax.fori_loop(0, groups // 2, fill, 0)

    sibling = (y0, par_of(z0, x0, 1 - c0))

    def core_copy(i):
        return remote(core_out.at[i], core_in.at[i], core_send.at[i], core_recv.at[i], sibling)

    x_steps = (1, NX - 1)

    def x_peer(side):
        return (y0, par_of(z0, lax.rem(x0 + x_steps[side], NX), c0))

    def relay_copy(i, side):
        return remote(r_out.at[i, side], r_in.at[i, side], r_send.at[i, side], r_recv.at[i, side], x_peer(side))

    def x_copy(i, side):
        return remote(x_out.at[i, side], x_in.at[i, side], x_send.at[i, side], x_recv.at[i, side], x_peer(side))

    def y_copy(i, d):
        peer = (lax.rem(y0 + d, ny), q0)
        return remote(y_out.at[i, d - 1], y_in.at[i, d - 1], y_send.at[i, d - 1], y_recv.at[i, d - 1], peer)

    def z_copy(i):
        peer = (y0, par_of(lax.rem(z0 + z_distance(i), nz), x0, c0))
        return remote(z_out.at[i], z_in.at[i], z_send.at[i], z_recv.at[i], peer)

    def yz_copy(dy):
        peer = (lax.rem(y0 + dy, ny), par_of(lax.rem(z0 + nz - 1, nz), x0, c0))
        return remote(yz_out.at[dy], yz_in.at[dy], yz_send.at[dy], yz_recv.at[dy], peer)

    def multiply(i, source):
        lhs = jnp.concatenate([g_ref[b] for b in range(groups)], axis=1)
        for pair in range(2):
            part = jnp.dot(lhs, source(pair), preferred_element_type=jnp.float32)
            for k in range(2):
                at = 2 * k * LANES
                own[i, pair * 2 + k] = part[:, at : at + LANES]
                core_out[i, pair * 2 + k] = part[:, at + LANES : at + 2 * LANES]
        core_copy(i).start()

    upper_rows = all_rows // 2

    def piece_of(rows, dy):
        e = lax.rem(y0 + dy, ny)
        trains = rows[pl.ds(pl.multiple_of(e * TRAIN_ROWS, TRAIN_ROWS), TRAIN_ROWS), :]
        return jnp.concatenate([trains, rows[all_train:, :]], axis=0)

    def after_core(i):
        core_copy(i).wait_recv()
        for k in range(NX):
            total = own[i, k] + core_in[i, k]
            if order[k] == 2:
                r_out[i, 0] = total[:upper_rows].astype(jnp.bfloat16)
                r_out[i, 1] = total[upper_rows:].astype(jnp.bfloat16)
                relay_copy(i, 0).start()
                relay_copy(i, 1).start()
            else:
                own[i, k] = total

    def after_relay(i):
        for side in range(2):
            relay_copy(i, side).wait_recv()
            total = own[i, order.index(x_steps[side])]
            parts = [total[:upper_rows], total[upper_rows:]]
            parts[side] = parts[side] + r_in[i, side].astype(jnp.float32)
            x_out[i, side] = jnp.concatenate(parts, axis=0).astype(jnp.bfloat16)
            x_copy(i, side).start()

    def after_x(i):
        total = own[i, order.index(0)]
        for side in range(2):
            x_copy(i, side).wait_recv()
            total = total + x_in[i, side].astype(jnp.float32)
        x_sum[...] = total

        @pl.when(i != nz - 2)
        def _():
            for d in range(1, ny):
                y_out[i, d - 1] = piece_of(x_sum, d).astype(jnp.bfloat16)
                y_copy(i, d).start()
            y_own[i] = piece_of(x_sum, 0)

        @pl.when(i == nz - 2)
        def _():
            for dy in (2, 1, 3, 0):
                yz_out[dy] = piece_of(x_sum, dy).astype(jnp.bfloat16)
                yz_copy(dy).start()

    def y_total(i):
        total = y_own[i]
        for d in range(1, ny):
            y_copy(i, d).wait_recv()
            total = total + y_in[i, d - 1].astype(jnp.float32)
        return total

    def after_y(i):
        z_out[i] = y_total(i)
        z_copy(i).start()

    def stage(i, lag, work, count):
        @pl.when((i >= lag) & (i < lag + count))
        def _():
            work(i - lag)

    def passed_on(i):
        stage(i, CORE_LAG, after_core, nz)
        stage(i, RELAY_LAG, after_relay, nz)
        stage(i, Y_LAG, after_y, nz - 2)
        stage(i, X_LAG, after_x, nz)

    mix_from = 0

    def with_gen(i, carry):
        for k in range(2):
            generate(gen_first + (i - mix_from) * 2 + k, late_tiles, (i - mix_from) * 2 + k)
        multiply(i, lambda pair: tiles[i * 2 + pair])
        passed_on(i)
        return carry

    def without_gen(i, carry):
        multiply(i, lambda pair: tiles[i * 2 + pair])
        passed_on(i)
        return carry

    def rest(i, carry):
        passed_on(i)
        return carry

    gen_steps = (nz * NX - gen_first) // 2
    lax.fori_loop(mix_from, mix_from + gen_steps, with_gen, 0)
    lax.fori_loop(mix_from + gen_steps, nz - 2, without_gen, 0)
    for i in (nz - 2, nz - 1):
        multiply(i, lambda pair: late_tiles[(i - nz + 2) * 2 + pair])
        passed_on(jnp.int32(i))
    lax.fori_loop(nz, nz - 2 + Y_LAG, rest, 0)
    total = y_total(nz - 1)
    for i in range(nz - 2):
        z_copy(i).wait_recv()
        total = total + z_in[i]
    for dy in range(ny):
        yz_copy(dy).wait_recv()
        total = total + yz_in[dy].astype(jnp.float32)

    total = total * (1.0 / math.sqrt(P_SIZE))
    trains, vals = total[:TRAIN_ROWS], total[TRAIN_ROWS:]
    fold = LANES // all_val
    wide = jnp.concatenate([vals] * fold, axis=0)
    dims = (((1,), (1,)), ((), ()))
    inner = lax.dot_general(trains, wide, dims, precision=lax.Precision.HIGHEST, preferred_element_type=jnp.float32)
    by_row = jnp.broadcast_to(jnp.sum(vals * vals, axis=1, keepdims=True), (all_val, LANES))
    row = lax.broadcasted_iota(jnp.int32, (all_val, LANES), 0)
    lane = lax.broadcasted_iota(jnp.int32, (all_val, LANES), 1)
    val_sq = jnp.sum(jnp.where(lax.rem(lane, all_val) == row, by_row, 0.0), axis=0, keepdims=True)
    val_sq = jnp.broadcast_to(val_sq, (8, LANES))
    train_sq = jnp.broadcast_to(jnp.sum(trains * trains, axis=1, keepdims=True), (TRAIN_ROWS, LANES))
    block = lax.broadcasted_iota(jnp.int32, (8, LANES), 1) // all_val

    def packed(a):
        out = a[:8]
        for b in range(1, TRAIN_ROWS // 8):
            out = jnp.where(block == b, a[b * 8 : (b + 1) * 8], out)
        return out

    def share(message, out_ref, in_ref, send, recv, targets, meanwhile):
        out_ref[...] = message
        copies = [
            remote(out_ref, in_ref.at[n], send.at[n], recv.at[n], target) for n, target in enumerate(targets)
        ]
        for copy in copies:
            copy.start()
        meanwhile()
        for n, copy in enumerate(copies):
            copy.wait_recv()
            message = message + in_ref[n]
        return message, copies

    def all_sent():
        for d in range(1, ny):
            train_copy(d, y0).wait_send()
            val_copy(d, y0).wait_send()

        def sent(i, carry):
            core_copy(i).wait_send()
            for side in range(2):
                relay_copy(i, side).wait_send()
                x_copy(i, side).wait_send()
            return carry

        def yz_sent(i, carry):
            for d in range(1, ny):
                y_copy(i, d).wait_send()
            z_copy(i).wait_send()
            return carry

        lax.fori_loop(0, nz, sent, 0)
        lax.fori_loop(0, nz - 2, yz_sent, 0)
        for d in range(1, ny):
            y_copy(nz - 1, d).wait_send()
        for dy in range(ny):
            yz_copy(dy).wait_send()

    part = all_val // 2
    lower, odd = lane_masks(all_val)
    squares = jnp.where(lower, packed(train_sq), jnp.where(odd, val_sq, turned(val_sq, part)))
    message = jnp.concatenate([packed(inner), squares], axis=0)
    near = [(y0, par_of(z0, lax.rem(x0 + d, NX), c)) for d in range(NX) for c in (c0, 1 - c0)][1:]
    message, copies1 = share(message, g1_out, g1_in, g1_send, g1_recv, near, all_sent)
    far = [(y0, par_of(lax.rem(z0 + d, nz), x0, c0)) for d in range(1, nz)]
    message, copies2 = share(message, g2_out, g2_in, g2_send, g2_recv, far, lambda: None)
    raw_ref[...] = trains
    message_ref[...] = message
    for copy in copies1 + copies2:
        copy.wait_send()


def per_device(ny, par, train, val, m1, m2, rows, cols, off):
    nz = par // (NX * NC)
    local = train.shape[1]
    depth = local // ny
    all_rows = ny * (TRAIN_ROWS + VAL_ROWS)
    piece = TRAIN_ROWS + ny * VAL_ROWS
    tiles = nz * NX
    gen_early, gen_first = 6, tiles - 8
    vmem = pl.BlockSpec(memory_space=pltpu.VMEM)
    f32, bf16 = jnp.float32, jnp.bfloat16
    dma = pltpu.SemaphoreType.DMA
    raw, message = pl.pallas_call(
        functools.partial(kernel, ny, nz, gen_early, gen_first),
        out_shape=(
            jax.ShapeDtypeStruct((TRAIN_ROWS, LANES), f32),
            jax.ShapeDtypeStruct((16, LANES), f32),
        ),
        in_specs=[pl.BlockSpec(memory_space=pl.ANY)] + [vmem] * 5 + [pl.BlockSpec(memory_space=pltpu.SMEM)],
        out_specs=(vmem, vmem),
        scratch_shapes=[
            pltpu.VMEM((depth, LANES), jnp.int32),
            pltpu.VMEM((ny, TRAIN_ROWS, depth), bf16),
            pltpu.VMEM((ny - 1, 2 * VAL_ROWS, depth // 2), bf16),
            pltpu.VMEM((ny, 2 * VAL_ROWS, depth // 2), bf16),
            pltpu.VMEM((depth // LANES, all_rows, LANES), bf16),
            pltpu.VMEM((tiles // 2 - 4, depth, 4 * LANES), bf16),
            pltpu.VMEM((4, depth, 4 * LANES), bf16),
            pltpu.VMEM((nz, NX, all_rows, LANES), f32),
            pltpu.VMEM((nz, NX, all_rows, LANES), f32),
            pltpu.VMEM((nz, NX, all_rows, LANES), f32),
            pltpu.VMEM((nz, 2, all_rows // 2, LANES), bf16),
            pltpu.VMEM((nz, 2, all_rows // 2, LANES), bf16),
            pltpu.VMEM((nz, 2, all_rows, LANES), bf16),
            pltpu.VMEM((nz, 2, all_rows, LANES), bf16),
            pltpu.VMEM((all_rows, LANES), f32),
            pltpu.VMEM((nz, ny - 1, piece, LANES), bf16),
            pltpu.VMEM((nz, ny - 1, piece, LANES), bf16),
            pltpu.VMEM((nz, piece, LANES), f32),
            pltpu.VMEM((nz - 2, piece, LANES), f32),
            pltpu.VMEM((nz - 2, piece, LANES), f32),
            pltpu.VMEM((ny, piece, LANES), bf16),
            pltpu.VMEM((ny, piece, LANES), bf16),
            pltpu.VMEM((16, LANES), f32),
            pltpu.VMEM((NX * NC - 1, 16, LANES), f32),
            pltpu.VMEM((16, LANES), f32),
            pltpu.VMEM((nz - 1, 16, LANES), f32),
            dma((2, ny - 1)), dma((2, ny - 1)), dma,
            dma((nz,)), dma((nz,)),
            dma((nz, 2)), dma((nz, 2)),
            dma((nz, 2)), dma((nz, 2)),
            dma((nz, ny - 1)), dma((nz, ny - 1)),
            dma((nz - 2,)), dma((nz - 2,)),
            dma((ny,)), dma((ny,)),
            dma((NX * NC - 1,)), dma((NX * NC - 1,)),
            dma((nz - 1,)), dma((nz - 1,)),
        ],
        compiler_params=pltpu.CompilerParams(
            collective_id=0, has_side_effects=True, vmem_limit_bytes=60 << 20
        ),
        name="project",
    )(
        train, val, m1.reshape(1, local), m2.reshape(1, local),
        rows.reshape(local // LANES, LANES), cols.reshape(1, cols.shape[0]), off,
    )
    return pl.pallas_call(
        functools.partial(finish, ny * VAL_ROWS),
        out_shape=(
            jax.ShapeDtypeStruct((TRAIN_ROWS, LANES), f32),
            jax.ShapeDtypeStruct((TRAIN_ROWS, ny * VAL_ROWS), f32),
        ),
        in_specs=[vmem, vmem],
        out_specs=(vmem, vmem),
        name="finish",
    )(raw, message)


def solution(mesh):
    in_specs = (P("ex", "par"), P("ex", "par"), P("par"), P("par"), P("par"), P(), P())
    out_specs = (P("ex", "par"), P("ex", None))
    body = functools.partial(per_device, mesh.shape["ex"], mesh.shape["par"])
    return jax.shard_map(body, mesh=mesh, in_specs=in_specs, out_specs=out_specs, check_vma=False)
```

```python
import functools
import math

import jax
import jax.numpy as jnp
from jax import lax
from jax.experimental import pallas as pl
from jax.experimental.pallas import tpu as pltpu
from jax.sharding import PartitionSpec as P

K = 8192
P_SIZE = 524288
MESH = pl.DeviceIdType.MESH
LANES = 128
NX = 4
NC = 2
TRAIN_ROWS = 32
VAL_ROWS = 8
SIGN_FACTOR = ((739982445 << 15) + 2**31) % 2**32 - 2**31
CORE_LAG, RELAY_LAG, X_LAG, Y_LAG = 1, 3, 6, 9


def make_entries(row_b, cols, offset, dest, depth, start):
    step = 128
    for first in range(0, depth, step):
        rows = row_b[first : first + step, :]
        for half, col in enumerate(cols):
            mixed = rows * col + offset
            mixed = mixed ^ (mixed >> 15)
            mixed = mixed * SIGN_FACTOR
            dest[first : first + step, pl.ds(pl.multiple_of(start + half * LANES, LANES), LANES)] = jnp.where(
                mixed < 0, jnp.bfloat16(1), jnp.bfloat16(-1)
            )


def turned(a, by):
    return jnp.concatenate([a[:, LANES - by :], a[:, : LANES - by]], axis=1)


def lane_masks(width):
    lane = lax.broadcasted_iota(jnp.int32, (8, LANES), 1)
    return lax.rem(lane, width) < width // 2, lax.rem(lane // width, 2) == 1


def finish(all_val, raw_ref, message_ref, feat_ref, scores_ref):
    part = all_val // 2
    lower, odd = lane_masks(all_val)
    inverse = lax.rsqrt(message_ref[8:] / K + 1e-06)
    before = turned(inverse, part)
    train_inv = jnp.where(lower, inverse, before)
    val_inv = jnp.where(
        odd, jnp.where(lower, before, inverse),
        jnp.where(lower, turned(inverse, LANES - part), turned(inverse, LANES - 2 * part)),
    )
    scores = message_ref[:8] * train_inv * val_inv * (1.0 / K)
    for b in range(TRAIN_ROWS // 8):
        at = slice(b * 8, (b + 1) * 8)
        scores_ref[at, :] = scores[:, b * all_val : (b + 1) * all_val]
        scale = jnp.broadcast_to(train_inv[:, b * all_val : b * all_val + 1], (8, LANES))
        feat_ref[at, :] = raw_ref[at, :] * scale


def kernel(
    ny, nz, gen_early, gen_first,
    train_ref, val_ref, m1_ref, m2_ref, rows_ref, cols_ref, off_ref,
    raw_ref, message_ref,
    row_b, train_in, val_out, val_in, g_ref, tiles, late_tiles,
    core_out, core_in, own, r_out, r_in, x_out, x_in, x_sum, y_out, y_in, y_own, z_out, z_in, yz_out, yz_in,
    g1_out, g1_in, g2_out, g2_in,
    in_send, in_recv, in_local, core_send, core_recv, r_send, r_recv, x_send, x_recv, y_send, y_recv, z_send, z_recv, yz_send, yz_recv,
    g1_send, g1_recv, g2_send, g2_recv,
):
    y0 = lax.axis_index("ex")
    q0 = lax.axis_index("par")
    c0 = lax.rem(q0, NC)
    x0 = lax.rem(q0 // NC, NX)
    z0 = q0 // (NC * NX)
    depth = row_b.shape[0]
    all_train = ny * TRAIN_ROWS
    all_val = ny * VAL_ROWS
    all_rows = all_train + all_val
    piece = TRAIN_ROWS + all_val

    def par_of(z, x, c):
        return (z * NX + x) * NC + c

    peers = [(y0, par_of(z0, x0, 1 - c0))]
    peers += [(y0, par_of(z0, lax.rem(x0 + d, NX), c)) for d in range(1, NX) for c in (c0, 1 - c0)]
    peers += [(lax.rem(y0 + d, ny), q0) for d in range(1, ny)]
    peers += [(y0, par_of(lax.rem(z0 + d, nz), x0, c0)) for d in range(1, nz)]
    peers += [(lax.rem(y0 + d, ny), par_of(lax.rem(z0 + 1, nz), x0, c0)) for d in range(1, ny)]
    barrier = pltpu.get_barrier_semaphore()
    for peer in peers:
        pl.semaphore_signal(barrier, inc=1, device_id=peer, device_id_type=MESH)

    def remote(src, dst, send, recv, peer):
        return pltpu.make_async_remote_copy(
            src_ref=src, dst_ref=dst, send_sem=send, recv_sem=recv, device_id=peer, device_id_type=MESH
        )

    def train_copy(d, slot):
        e = lax.rem(y0 + d, ny)
        return remote(
            train_ref.at[:, pl.ds(pl.multiple_of(e * depth, LANES), depth)],
            train_in.at[slot], in_send.at[0, d - 1], in_recv.at[0, d - 1], (e, q0),
        )

    def val_copy(d, slot):
        e = lax.rem(y0 + d, ny)
        return remote(val_out.at[d - 1], val_in.at[slot], in_send.at[1, d - 1], in_recv.at[1, d - 1], (e, q0))

    groups = depth // LANES
    codes = rows_ref[pl.ds(pl.multiple_of(y0 * groups, groups), groups), :].T
    for j in range(groups):
        row_b[j * LANES : (j + 1) * LANES, :] = jnp.broadcast_to(codes[:, j : j + 1], (LANES, LANES))
    offset = off_ref[0]

    order = (2, 1, 3, 0)

    def z_distance(i):
        return nz // 2 + jnp.where(lax.rem(i, 2) == 0, i // 2, -((i + 1) // 2))

    def tile_features(t, step_in_chunk):
        z = lax.rem(z0 + z_distance(t), nz)
        x = lax.rem(x0 + step_in_chunk, NX)
        base = par_of(z, x, 0) * LANES
        mine = cols_ref[:, pl.ds(pl.multiple_of(base + c0 * LANES, LANES), LANES)]
        other = cols_ref[:, pl.ds(pl.multiple_of(base + (1 - c0) * LANES, LANES), LANES)]
        return mine, other

    def distance(k):
        return jnp.where(k == 0, 2, jnp.where(k == 1, 1, jnp.where(k == 2, 3, 0)))

    def generate(t, dest, at):
        cols = tile_features(t // NX, distance(lax.rem(t, NX)))
        make_entries(row_b, cols, offset, dest.at[at // 2], depth, lax.rem(at, 2) * (2 * LANES))

    half = depth // 2
    for d in range(ny):
        e = lax.rem(y0 + d, ny)
        upper = val_ref[:, pl.ds(pl.multiple_of(e * depth, LANES), half)].astype(jnp.float32)
        lower = val_ref[:, pl.ds(pl.multiple_of(e * depth + half, LANES), half)].astype(jnp.float32)
        stacked = jnp.concatenate([upper, lower], axis=0).astype(jnp.bfloat16)
        if d == 0:
            val_in[y0] = stacked
        else:
            val_out[d - 1] = stacked

    lax.fori_loop(0, gen_early, lambda t, c: (generate(t, tiles, t), c)[1], 0)
    pl.semaphore_wait(barrier, len(peers))
    for d in sorted(range(1, ny), key=lambda d: -min(d, ny - d)):
        train_copy(d, y0).start()
        val_copy(d, y0).start()
    local_copy = pltpu.make_async_copy(
        train_ref.at[:, pl.ds(pl.multiple_of(y0 * depth, LANES), depth)], train_in.at[y0], in_local
    )
    local_copy.start()

    lax.fori_loop(gen_early, gen_first, lambda t, c: (generate(t, tiles, t), c)[1], 0)

    local_copy.wait()
    for d in range(1, ny):
        source = lax.rem(y0 + ny - d, ny)
        train_copy(d, source).wait_recv()
        val_copy(d, source).wait_recv()

    def fill(j, carry):
        vals = [[], []]
        at = pl.ds(pl.multiple_of(j * LANES, LANES), LANES)
        for e in range(ny):
            both = val_in[e, :, at].astype(jnp.float32)
            vals[0].append(both[:VAL_ROWS])
            vals[1].append(both[VAL_ROWS:])
        for h in range(2):
            block = j + h * (groups // 2)
            here = pl.ds(pl.multiple_of(block * LANES, LANES), LANES)
            there = pl.ds(pl.multiple_of(y0 * depth + block * LANES, LANES), LANES)
            m1 = 0.9 * m1_ref[:, there]
            m2 = 0.999 * m2_ref[:, there]
            for e in range(ny):
                g = train_in[e, :, here].astype(jnp.float32)
                direction = (m1 + 0.1 * g) / (jnp.sqrt(m2 + 0.001 * g * g) + 1e-08)
                g_ref[block, e * TRAIN_ROWS : (e + 1) * TRAIN_ROWS, :] = direction.astype(jnp.bfloat16)
            g_ref[block, all_train:all_rows, :] = jnp.concatenate(vals[h], axis=0).astype(jnp.bfloat16)
        return carry

    lax.fori_loop(0, groups // 2, fill, 0)

    sibling = (y0, par_of(z0, x0, 1 - c0))

    def core_copy(i):
        return remote(core_out.at[i], core_in.at[i], core_send.at[i], core_recv.at[i], sibling)

    x_steps = (1, NX - 1)

    def x_peer(side):
        return (y0, par_of(z0, lax.rem(x0 + x_steps[side], NX), c0))

    def relay_copy(i, side):
        return remote(r_out.at[i, side], r_in.at[i, side], r_send.at[i, side], r_recv.at[i, side], x_peer(side))

    def x_copy(i, side):
        return remote(x_out.at[i, side], x_in.at[i, side], x_send.at[i, side], x_recv.at[i, side], x_peer(side))

    def y_copy(i, d):
        peer = (lax.rem(y0 + d, ny), q0)
        return remote(y_out.at[i, d - 1], y_in.at[i, d - 1], y_send.at[i, d - 1], y_recv.at[i, d - 1], peer)

    def z_copy(i):
        peer = (y0, par_of(lax.rem(z0 + z_distance(i), nz), x0, c0))
        return remote(z_out.at[i], z_in.at[i], z_send.at[i], z_recv.at[i], peer)

    def yz_copy(dy):
        peer = (lax.rem(y0 + dy, ny), par_of(lax.rem(z0 + nz - 1, nz), x0, c0))
        return remote(yz_out.at[dy], yz_in.at[dy], yz_send.at[dy], yz_recv.at[dy], peer)

    def multiply(i, source):
        lhs = jnp.concatenate([g_ref[b] for b in range(groups)], axis=1)
        for pair in range(2):
            part = jnp.dot(lhs, source(pair), preferred_element_type=jnp.float32)
            for k in range(2):
                at = 2 * k * LANES
                own[i, pair * 2 + k] = part[:, at : at + LANES]
                core_out[i, pair * 2 + k] = part[:, at + LANES : at + 2 * LANES]
        core_copy(i).start()

    upper_rows = all_rows // 2

    def piece_of(rows, dy):
        e = lax.rem(y0 + dy, ny)
        trains = rows[pl.ds(pl.multiple_of(e * TRAIN_ROWS, TRAIN_ROWS), TRAIN_ROWS), :]
        return jnp.concatenate([trains, rows[all_train:, :]], axis=0)

    def after_core(i):
        core_copy(i).wait_recv()
        for k in range(NX):
            total = own[i, k] + core_in[i, k]
            if order[k] == 2:
                r_out[i, 0] = total[:upper_rows].astype(jnp.bfloat16)
                r_out[i, 1] = total[upper_rows:].astype(jnp.bfloat16)
                relay_copy(i, 0).start()
                relay_copy(i, 1).start()
            else:
                own[i, k] = total

    def after_relay(i):
        for side in range(2):
            relay_copy(i, side).wait_recv()
            total = own[i, order.index(x_steps[side])]
            parts = [total[:upper_rows], total[upper_rows:]]
            parts[side] = parts[side] + r_in[i, side].astype(jnp.float32)
            x_out[i, side] = jnp.concatenate(parts, axis=0).astype(jnp.bfloat16)
            x_copy(i, side).start()

    def after_x(i):
        total = own[i, order.index(0)]
        for side in range(2):
            x_copy(i, side).wait_recv()
            total = total + x_in[i, side].astype(jnp.float32)
        x_sum[...] = total

        @pl.when(i != nz - 2)
        def _():
            for d in range(1, ny):
                y_out[i, d - 1] = piece_of(x_sum, d).astype(jnp.bfloat16)
                y_copy(i, d).start()
            y_own[i] = piece_of(x_sum, 0)

        @pl.when(i == nz - 2)
        def _():
            for dy in (2, 1, 3, 0):
                yz_out[dy] = piece_of(x_sum, dy).astype(jnp.bfloat16)
                yz_copy(dy).start()

    def y_total(i):
        total = y_own[i]
        for d in range(1, ny):
            y_copy(i, d).wait_recv()
            total = total + y_in[i, d - 1].astype(jnp.float32)
        return total

    def after_y(i):
        z_out[i] = y_total(i)
        z_copy(i).start()

    def stage(i, lag, work, count):
        @pl.when((i >= lag) & (i < lag + count))
        def _():
            work(i - lag)

    def passed_on(i):
        stage(i, CORE_LAG, after_core, nz)
        stage(i, RELAY_LAG, after_relay, nz)
        stage(i, Y_LAG, after_y, nz - 2)
        stage(i, X_LAG, after_x, nz)

    mix_from = 0

    def with_gen(i, carry):
        for k in range(2):
            generate(gen_first + (i - mix_from) * 2 + k, late_tiles, (i - mix_from) * 2 + k)
        multiply(i, lambda pair: tiles[i * 2 + pair])
        passed_on(i)
        return carry

    def without_gen(i, carry):
        multiply(i, lambda pair: tiles[i * 2 + pair])
        passed_on(i)
        return carry

    def rest(i, carry):
        passed_on(i)
        return carry

    gen_steps = (nz * NX - gen_first) // 2
    lax.fori_loop(mix_from, mix_from + gen_steps, with_gen, 0)
    lax.fori_loop(mix_from + gen_steps, nz - 2, without_gen, 0)
    for i in (nz - 2, nz - 1):
        multiply(i, lambda pair: late_tiles[(i - nz + 2) * 2 + pair])
        passed_on(jnp.int32(i))
    lax.fori_loop(nz, nz - 2 + Y_LAG, rest, 0)
    total = y_total(nz - 1)
    for i in range(nz - 2):
        z_copy(i).wait_recv()
        total = total + z_in[i]
    for dy in range(ny):
        yz_copy(dy).wait_recv()
        total = total + yz_in[dy].astype(jnp.float32)

    total = total * (1.0 / math.sqrt(P_SIZE))
    trains, vals = total[:TRAIN_ROWS], total[TRAIN_ROWS:]
    fold = LANES // all_val
    wide = jnp.concatenate([vals] * fold, axis=0)
    dims = (((1,), (1,)), ((), ()))
    inner = lax.dot_general(trains, wide, dims, precision=lax.Precision.HIGHEST, preferred_element_type=jnp.float32)
    by_row = jnp.broadcast_to(jnp.sum(vals * vals, axis=1, keepdims=True), (all_val, LANES))
    row = lax.broadcasted_iota(jnp.int32, (all_val, LANES), 0)
    lane = lax.broadcasted_iota(jnp.int32, (all_val, LANES), 1)
    val_sq = jnp.sum(jnp.where(lax.rem(lane, all_val) == row, by_row, 0.0), axis=0, keepdims=True)
    val_sq = jnp.broadcast_to(val_sq, (8, LANES))
    train_sq = jnp.broadcast_to(jnp.sum(trains * trains, axis=1, keepdims=True), (TRAIN_ROWS, LANES))
    block = lax.broadcasted_iota(jnp.int32, (8, LANES), 1) // all_val

    def packed(a):
        out = a[:8]
        for b in range(1, TRAIN_ROWS // 8):
            out = jnp.where(block == b, a[b * 8 : (b + 1) * 8], out)
        return out

    def share(message, out_ref, in_ref, send, recv, targets, meanwhile):
        out_ref[...] = message
        copies = [
            remote(out_ref, in_ref.at[n], send.at[n], recv.at[n], target) for n, target in enumerate(targets)
        ]
        for copy in copies:
            copy.start()
        meanwhile()
        for n, copy in enumerate(copies):
            copy.wait_recv()
            message = message + in_ref[n]
        return message, copies

    def all_sent():
        for d in range(1, ny):
            train_copy(d, y0).wait_send()
            val_copy(d, y0).wait_send()

        def sent(i, carry):
            core_copy(i).wait_send()
            for side in range(2):
                relay_copy(i, side).wait_send()
                x_copy(i, side).wait_send()
            return carry

        def yz_sent(i, carry):
            for d in range(1, ny):
                y_copy(i, d).wait_send()
            z_copy(i).wait_send()
            return carry

        lax.fori_loop(0, nz, sent, 0)
        lax.fori_loop(0, nz - 2, yz_sent, 0)
        for d in range(1, ny):
            y_copy(nz - 1, d).wait_send()
        for dy in range(ny):
            yz_copy(dy).wait_send()

    part = all_val // 2
    lower, odd = lane_masks(all_val)
    squares = jnp.where(lower, packed(train_sq), jnp.where(odd, val_sq, turned(val_sq, part)))
    message = jnp.concatenate([packed(inner), squares], axis=0)
    near = [(y0, par_of(z0, lax.rem(x0 + d, NX), c)) for d in range(NX) for c in (c0, 1 - c0)][1:]
    message, copies1 = share(message, g1_out, g1_in, g1_send, g1_recv, near, all_sent)
    far = [(y0, par_of(lax.rem(z0 + d, nz), x0, c0)) for d in range(1, nz)]
    message, copies2 = share(message, g2_out, g2_in, g2_send, g2_recv, far, lambda: None)
    raw_ref[...] = trains
    message_ref[...] = message
    for copy in copies1 + copies2:
        copy.wait_send()


def per_device(ny, par, train, val, m1, m2, rows, cols, off):
    nz = par // (NX * NC)
    local = train.shape[1]
    depth = local // ny
    all_rows = ny * (TRAIN_ROWS + VAL_ROWS)
    piece = TRAIN_ROWS + ny * VAL_ROWS
    tiles = nz * NX
    gen_early, gen_first = 7, tiles - 8
    vmem = pl.BlockSpec(memory_space=pltpu.VMEM)
    f32, bf16 = jnp.float32, jnp.bfloat16
    dma = pltpu.SemaphoreType.DMA
    raw, message = pl.pallas_call(
        functools.partial(kernel, ny, nz, gen_early, gen_first),
        out_shape=(
            jax.ShapeDtypeStruct((TRAIN_ROWS, LANES), f32),
            jax.ShapeDtypeStruct((16, LANES), f32),
        ),
        in_specs=[pl.BlockSpec(memory_space=pl.ANY)] + [vmem] * 5 + [pl.BlockSpec(memory_space=pltpu.SMEM)],
        out_specs=(vmem, vmem),
        scratch_shapes=[
            pltpu.VMEM((depth, LANES), jnp.int32),
            pltpu.VMEM((ny, TRAIN_ROWS, depth), bf16),
            pltpu.VMEM((ny - 1, 2 * VAL_ROWS, depth // 2), bf16),
            pltpu.VMEM((ny, 2 * VAL_ROWS, depth // 2), bf16),
            pltpu.VMEM((depth // LANES, all_rows, LANES), bf16),
            pltpu.VMEM((tiles // 2 - 4, depth, 4 * LANES), bf16),
            pltpu.VMEM((4, depth, 4 * LANES), bf16),
            pltpu.VMEM((nz, NX, all_rows, LANES), f32),
            pltpu.VMEM((nz, NX, all_rows, LANES), f32),
            pltpu.VMEM((nz, NX, all_rows, LANES), f32),
            pltpu.VMEM((nz, 2, all_rows // 2, LANES), bf16),
            pltpu.VMEM((nz, 2, all_rows // 2, LANES), bf16),
            pltpu.VMEM((nz, 2, all_rows, LANES), bf16),
            pltpu.VMEM((nz, 2, all_rows, LANES), bf16),
            pltpu.VMEM((all_rows, LANES), f32),
            pltpu.VMEM((nz, ny - 1, piece, LANES), bf16),
            pltpu.VMEM((nz, ny - 1, piece, LANES), bf16),
            pltpu.VMEM((nz, piece, LANES), f32),
            pltpu.VMEM((nz - 2, piece, LANES), f32),
            pltpu.VMEM((nz - 2, piece, LANES), f32),
            pltpu.VMEM((ny, piece, LANES), bf16),
            pltpu.VMEM((ny, piece, LANES), bf16),
            pltpu.VMEM((16, LANES), f32),
            pltpu.VMEM((NX * NC - 1, 16, LANES), f32),
            pltpu.VMEM((16, LANES), f32),
            pltpu.VMEM((nz - 1, 16, LANES), f32),
            dma((2, ny - 1)), dma((2, ny - 1)), dma,
            dma((nz,)), dma((nz,)),
            dma((nz, 2)), dma((nz, 2)),
            dma((nz, 2)), dma((nz, 2)),
            dma((nz, ny - 1)), dma((nz, ny - 1)),
            dma((nz - 2,)), dma((nz - 2,)),
            dma((ny,)), dma((ny,)),
            dma((NX * NC - 1,)), dma((NX * NC - 1,)),
            dma((nz - 1,)), dma((nz - 1,)),
        ],
        compiler_params=pltpu.CompilerParams(
            collective_id=0, has_side_effects=True, vmem_limit_bytes=60 << 20
        ),
        name="project",
    )(
        train, val, m1.reshape(1, local), m2.reshape(1, local),
        rows.reshape(local // LANES, LANES), cols.reshape(1, cols.shape[0]), off,
    )
    return pl.pallas_call(
        functools.partial(finish, ny * VAL_ROWS),
        out_shape=(
            jax.ShapeDtypeStruct((TRAIN_ROWS, LANES), f32),
            jax.ShapeDtypeStruct((TRAIN_ROWS, ny * VAL_ROWS), f32),
        ),
        in_specs=[vmem, vmem],
        out_specs=(vmem, vmem),
        name="finish",
    )(raw, message)


def solution(mesh):
    in_specs = (P("ex", "par"), P("ex", "par"), P("par"), P("par"), P("par"), P(), P())
    out_specs = (P("ex", "par"), P("ex", None))
    body = functools.partial(per_device, mesh.shape["ex"], mesh.shape["par"])
    return jax.shard_map(body, mesh=mesh, in_specs=in_specs, out_specs=out_specs, check_vma=False)
```
